128 devices in a mesh: group: 4 (over y), dp: 32 (over x, z, core).
Axes of the slice: x: 4, y: 4, z: 4, core: 2. Of those that a mesh axis runs over, the one named last changes fastest.
Arguments:
- question_vectors: bfloat16 [16384, 2048], P(('group', 'dp')), may hold values from -0.5 to 0.5
- passages: bfloat16 [8192, 2048], P(('group', 'dp')), may hold values from -0.5 to 0.5
- positive: int32 [16384], P(('group', 'dp')), may hold values from 0 to 2047
- hard_owner: int32 [16384, 16], P(('group', 'dp')), may hold values from 0 to 127, as said below
- hard_row: int32 [16384, 16], P(('group', 'dp')), may hold values from 0 to 63
Outputs:
- loss: float32 [16384], P(('group', 'dp'))
- query_grad: bfloat16 [16384, 2048], P(('group', 'dp'))
- passage_grad: bfloat16 [8192, 2048], P(('group', 'dp'))
The draws below stay inside these ranges and needn't reach their ends.
Inputs may be any that keep to these rules, and one draw needn't show every extreme that they name: `hard_owner`: each query's 16 owners are different devices. Within one device's 128 queries one owner, the same for every device, is named by exactly 18 of them, and every other owner by at most 16.
All inputs are finite; a program needn't handle non-finite values.
Results may differ from the reference program's by a relative error of at most 0.02.
Values may be sent and summed in bfloat16 or wider, within the bound.
No kernel may reach another device: no remote copies, remote signals or barrier semaphores. Data moves between devices by JAX's collectives and lax.ppermute only.
A program may use at most 128 MiB of HBM per device.

```python
import jax
import jax.numpy as jnp
from jax import lax

D = 2048
Q_DEV = 128
HARD = 16
P_DEV = 64
MEAN_LOAD = 16
HARD_CAP = 18
GROUP_ROWS = 4096
GROUP_PASS = 2048
QUERIES = 16384
PASSAGES = 8192
N_GROUP = 4
N_DP = 32
DEVICES = 128


normalizer_heat = 0.02


def shared_normal(key):
    return jax.random.normal(jax.random.fold_in(key, 11), (PASSAGES, D), jnp.float32) / jnp.sqrt(D * 1.0)


def order_devices(single):
    return jax.random.permutation(single, DEVICES)


def order_queries(single):
    return jax.random.permutation(single, Q_DEV)


def order_slots(single):
    return jax.random.permutation(single, HARD)


def route_ids(key):
    seeded = jax.random.fold_in(key, 21)
    positive = jax.random.randint(jax.random.fold_in(seeded, 1), (QUERIES,), 0, GROUP_PASS, jnp.int32)
    passage_rows = jax.random.randint(jax.random.fold_in(seeded, 2), (QUERIES, HARD), 0, P_DEV, jnp.int32)
    busiest = jax.random.randint(jax.random.fold_in(seeded, 3), (), 0, DEVICES, jnp.int32)
    orders = jax.vmap(order_devices)(jax.random.split(jax.random.fold_in(seeded, 4), DEVICES)).astype(jnp.int32)
    leading = orders[:, 0:1]
    orders = jnp.where(orders == busiest, leading, orders)
    orders = orders.at[:, 0].set(busiest)
    positions = (jnp.arange(Q_DEV, dtype=jnp.int32)[:, None] * HARD + jnp.arange(HARD, dtype=jnp.int32)[None, :]) % DEVICES
    owners = jnp.take(orders, positions, axis=1)
    holding = jnp.any(positions == 0, axis=1)
    without = jnp.logical_not(holding).astype(jnp.int32)
    ranking = jnp.cumsum(without) - 1
    surplus = HARD_CAP - MEAN_LOAD
    altered = (without == 1) & (ranking < surplus)
    owners = owners.at[:, :, 0].set(jnp.where(altered[None, :], busiest, owners[:, :, 0]))
    shuffle = jax.vmap(order_queries)(jax.random.split(jax.random.fold_in(seeded, 5), DEVICES)).astype(jnp.int32)
    owners = jnp.take_along_axis(owners, shuffle[:, :, None], axis=1)
    mixing = jax.vmap(order_slots)(jax.random.split(jax.random.fold_in(seeded, 6), QUERIES)).astype(jnp.int32)
    owners = jnp.take_along_axis(owners.reshape(QUERIES, HARD), mixing, axis=1)
    return (positive, owners, passage_rows)


def draw_positive(key, part):
    positive, owners, passage_rows = route_ids(key)
    key = jax.random.fold_in(key, 7)
    return positive


def draw_hard_owner(key, part):
    positive, owners, passage_rows = route_ids(key)
    key = jax.random.fold_in(key, 8)
    return owners


def draw_hard_row(key, part):
    positive, owners, passage_rows = route_ids(key)
    key = jax.random.fold_in(key, 9)
    return passage_rows


def draw_question_vectors(key, part):
    positive, owners, passage_rows = route_ids(key)
    vector_width = shared_normal(key)
    key = jax.random.fold_in(key, 3)
    indices = jnp.arange(QUERIES, dtype=jnp.int32)
    groups = indices // GROUP_ROWS
    correct_column = groups * GROUP_PASS + positive
    hard_ids = owners * P_DEV + passage_rows
    highest_score = jax.random.uniform(jax.random.fold_in(key, 1), (QUERIES,), jnp.float32, 7.0, 10.0)
    score_differences = jax.random.uniform(jax.random.fold_in(key, 2), (QUERIES, HARD), jnp.float32, 1.5, 4.5)
    random_perturbation = jax.random.normal(jax.random.fold_in(key, 4), (QUERIES, D), jnp.float32) / jnp.sqrt(D * 1.0)
    objective_value = (normalizer_heat * highest_score)[:, None] * jnp.take(vector_width, correct_column, axis=0) + 0.3 * random_perturbation
    for inbatch_position in range(HARD):
        rescale_multiplier = normalizer_heat * (highest_score - score_differences[:, inbatch_position])
        objective_value = objective_value + rescale_multiplier[:, None] * jnp.take(vector_width, hard_ids[:, inbatch_position], axis=0)
    return jnp.clip(objective_value, -0.5, 0.5).astype(jnp.bfloat16)


def draw_passages(key, part):
    objective_value = shared_normal(key)
    key = jax.random.fold_in(key, 5)
    return jnp.clip(objective_value, -0.5, 0.5).astype(jnp.bfloat16)


def setup_inputs(seed: int = 0) -> dict:
    seeds = jax.random.split(jax.random.key(seed), 6)
    question_vectors = draw_question_vectors(jax.random.fold_in(seeds[5], 71), 0)
    passages = draw_passages(jax.random.fold_in(seeds[5], 71), 0)
    positive = draw_positive(jax.random.fold_in(seeds[5], 71), 0)
    hard_owner = draw_hard_owner(jax.random.fold_in(seeds[5], 71), 0)
    hard_row = draw_hard_row(jax.random.fold_in(seeds[5], 71), 0)
    return {"question_vectors": question_vectors, "passages": passages, "positive": positive, "hard_owner": hard_owner, "hard_row": hard_row}


normalizer_heat = 0.02


def reference(question_vectors, passages, positive, hard_owner, hard_row):
    hard_ids = hard_owner * P_DEV + hard_row
    sharpness_multiplier = 1.0 / normalizer_heat
    query_groups = question_vectors.reshape(N_GROUP, GROUP_ROWS, D)
    passage_groups = passages.reshape(N_GROUP, GROUP_PASS, D)
    positive_groups = positive.reshape(N_GROUP, GROUP_ROWS)
    hard_groups = hard_ids.reshape(N_GROUP, GROUP_ROWS, HARD)

    def one_group(operands):
        question_tile, document_tile, pos_block, id_block = operands
        mined_negative_tile = passages[id_block]
        inbatch_scores = jnp.dot(question_tile, document_tile.T, preferred_element_type=jnp.float32) * sharpness_multiplier
        mined_scores = jnp.einsum("gi,gni->gn", question_tile.astype(jnp.float32), mined_negative_tile.astype(jnp.float32)) * sharpness_multiplier
        top = jnp.maximum(jnp.max(inbatch_scores, axis=1), jnp.max(mined_scores, axis=1))
        total = jnp.sum(jnp.exp(inbatch_scores - top[:, None]), axis=1) + jnp.sum(jnp.exp(mined_scores - top[:, None]), axis=1)
        log_partition = top + jnp.log(total)
        indicator_matrix = (pos_block[:, None] == jnp.arange(GROUP_PASS, dtype=jnp.int32)[None, :]).astype(jnp.float32)
        loss = log_partition - jnp.sum(inbatch_scores * indicator_matrix, axis=1)
        inbatch_weights = ((jnp.exp(inbatch_scores - log_partition[:, None]) - indicator_matrix) * sharpness_multiplier).astype(jnp.bfloat16)
        mined_weights = (jnp.exp(mined_scores - log_partition[:, None]) * sharpness_multiplier).astype(jnp.bfloat16)
        query_grad = jnp.dot(inbatch_weights, document_tile, preferred_element_type=jnp.float32)
        query_grad = query_grad + jnp.einsum("qk,qkd->qd", mined_weights.astype(jnp.float32), mined_negative_tile.astype(jnp.float32))
        coef_parts = inbatch_weights.reshape(N_DP, Q_DEV, GROUP_PASS).astype(jnp.float32)
        query_parts = question_tile.reshape(N_DP, Q_DEV, D).astype(jnp.float32)
        partial_sums = jnp.einsum("nqp,nqd->npd", coef_parts, query_parts)
        rounded = lax.optimization_barrier(partial_sums.astype(jnp.bfloat16))
        batch_grad = jnp.sum(rounded.astype(jnp.float32), axis=0)
        hard_term = (mined_weights.astype(jnp.float32)[:, :, None] * question_tile.astype(jnp.float32)[:, None, :]).astype(jnp.bfloat16)
        return loss, query_grad.astype(jnp.bfloat16), batch_grad, hard_term

    loss, query_grad, batch_grad, hard_term = lax.map(one_group, (query_groups, passage_groups, positive_groups, hard_groups))
    hard_grad = jnp.zeros((PASSAGES, D), jnp.float32).at[hard_ids.reshape(-1)].add(hard_term.reshape(-1, D).astype(jnp.float32))
    passage_grad = (batch_grad.reshape(PASSAGES, D) + hard_grad).astype(jnp.bfloat16)
    return loss.reshape(QUERIES), query_grad.reshape(QUERIES, D), passage_grad
```

```python
import jax
import jax.numpy as jnp
from jax import lax
from jax.sharding import PartitionSpec as P

HARD = 16
AXES = ("group", "dp")
SHARP = 1.0 / 0.02
FLOOR = -1e30
BF = jnp.bfloat16
F32 = jnp.float32


def index(y, x, z, c):
    return (((y % 4) * 4 + x % 4) * 4 + z % 4) * 2 + c % 2


def pairs(step):
    found = []
    for y in range(4):
        for x in range(4):
            for z in range(4):
                for c in range(2):
                    found.append((index(y, x, z, c), index(*step(y, x, z, c))))
    return found


def first(d):
    return pairs(lambda y, x, z, c: (y, x, z + d, c) if c else (y, x + d, z, c))


def second(d):
    return pairs(lambda y, x, z, c: (y, x + d, z, c) if c else (y, x, z + d, c))


def along(d):
    return pairs(lambda y, x, z, c: (y - d, x, z, c) if c else (y + d, x, z, c))


CORE = pairs(lambda y, x, z, c: (y, x, z, 1 - c))


def send(v, perm):
    return lax.ppermute(v, AXES, perm)


def join(*v):
    return jnp.concatenate(v, axis=0)


def spread(block, axis):
    h = block.shape[0] // 2
    up = send(block, axis(1))
    down = send(block, axis(-1))
    return block, up, send(up[:h], axis(1)), send(down[h:], axis(-1)), down


def fold(chunks, axis):
    h = chunks[0].shape[0] // 2
    low = [c.astype(BF) for c in chunks]
    up = send(low[2][:h], axis(-1))
    down = send(low[2][h:], axis(1))
    one = join((chunks[1][:h] + up.astype(F32)).astype(BF), low[1][h:])
    three = join(low[3][:h], (chunks[3][h:] + down.astype(F32)).astype(BF))
    return chunks[0] + send(one, axis(-1)).astype(F32) + send(three, axis(1)).astype(F32)


def merge(a, b):
    top = jnp.maximum(a[0], b[0])
    total = a[1] * jnp.exp(a[0] - top) + b[1] * jnp.exp(b[0] - top)
    return top, total, a[2] + b[2]


def local(question_vectors, passages, positive, hard_owner, hard_row):
    width = question_vectors.shape[1]
    group = lax.axis_index("group")
    dp = lax.axis_index("dp")
    core = dp % 2
    z = dp // 2 % 4
    x = dp // 8

    owner_rows = hard_owner.T.astype(BF)
    row_rows = hard_row.T.astype(BF)
    pos_rows = jnp.pad(jnp.stack([positive // 64, positive % 64]), ((0, 14), (0, 0))).astype(BF)
    meta = jnp.concatenate([owner_rows, row_rows, pos_rows], axis=1)
    meta = jnp.pad(meta, ((0, 0), (0, width - meta.shape[1])))
    mine = [join(question_vectors, meta)]
    for _ in range(3):
        mine.append(send(mine[-1], along(1)))
    theirs = [send(v, CORE) for v in mine]
    tiles = mine + theirs
    q = join(*[t[:128] for t in tiles])
    owners = jnp.concatenate([t[128:144, :128] for t in tiles], axis=1).astype(F32)
    rows = jnp.concatenate([t[128:144, 128:256] for t in tiles], axis=1).astype(F32)
    pos = jnp.concatenate([tiles[0][128:130, 256:384], tiles[4][128:130, 256:384]], axis=1).astype(F32)

    keep = lax.dynamic_slice_in_dim(passages, core * 32, 32, 0)
    give = lax.dynamic_slice_in_dim(passages, (1 - core) * 32, 32, 0)
    block = join(keep, send(give, CORE))
    plane = join(*spread(block, first))
    p = join(*spread(plane, second))

    far = jnp.arange(32, dtype=jnp.int32)
    k2, k1, b = far // 8, far // 2 % 4, far % 2
    kx = jnp.where(core == 0, k1, k2)
    kz = jnp.where(core == 0, k2, k1)
    local_id = ((x - kx + 4) % 4 * 4 + (z - kz + 4) % 4) * 2 + (core + b) % 2
    whole_id = group * 32 + local_id
    base = (core * 32 - 1).astype(F32)
    hit = owners[None] == whole_id.astype(F32)[:, None, None]
    hard_place = jnp.sum(jnp.where(hit, rows[None] - base, 0.0), axis=1)
    pos_place = jnp.where(pos[0][None] == local_id.astype(F32)[:, None], pos[1][None] - base, 0.0)
    step = jnp.arange(1, 33, dtype=jnp.int32).astype(F32)
    hard_hit = (hard_place[:, None, :] == step[None, :, None]).reshape(1024, 1024).astype(F32)
    pos_hit = (pos_place[:, None, :] == step[None, :, None]).reshape(1024, 256).astype(F32)

    scores = lax.dot_general(p, q, (((1,), (1,)), ((), ())), preferred_element_type=F32) * SHARP
    column = jnp.arange(1024, dtype=jnp.int32)
    inside = (column % 512 < 128).astype(F32)[None]
    weight = hard_hit + inside
    onehot = jnp.concatenate(
        [jnp.pad(pos_hit[:, :128], ((0, 0), (0, 384))), jnp.pad(pos_hit[:, 128:], ((0, 0), (0, 384)))], axis=1
    )
    masked = jnp.where(weight > 0, scores, FLOOR)
    top = jnp.max(masked, axis=0)
    total = jnp.sum(weight * jnp.exp(masked - top[None]), axis=0)
    chosen = jnp.sum(onehot * scores, axis=0)

    def unpack(v):
        return v[0], v[1], v[2]

    stats = jnp.pad(jnp.stack([top, total, chosen]), ((0, 5), (0, 0)))
    other = jnp.roll(send(stats, CORE), 512, axis=1)
    stats = jnp.pad(jnp.stack(merge(unpack(stats), unpack(other))), ((0, 5), (0, 0)))
    acc = unpack(stats)
    for t in range(1, 4):
        got = send(stats, along(t))
        got = jnp.concatenate(
            [jnp.roll(got[:, :512], 128 * t, axis=1), jnp.roll(got[:, 512:], -128 * t, axis=1)], axis=1
        )
        acc = merge(acc, unpack(got))
    lse = acc[0] + jnp.log(acc[1])
    loss = lse[:128] - acc[2][:128]

    coef = ((weight * jnp.exp(masked - lse[None]) - onehot) * SHARP).astype(BF)
    pg = jnp.dot(coef, q, preferred_element_type=F32)
    parts = fold([pg[256 * k : 256 * k + 256] for k in range(4)], second)
    parts = fold([parts[64 * k : 64 * k + 64] for k in range(4)], first)
    swapped = send(parts[32:].astype(BF), CORE)
    kept = parts[:32].astype(BF)
    passage_grad = jnp.where(core == 0, join(kept, swapped), join(swapped, kept))

    qg = lax.dot_general(coef, p, (((0,), (0,)), ((), ())), preferred_element_type=F32)
    qm = qg[:512] + send(qg[512:].astype(BF), CORE).astype(F32)
    run = qm[384:]
    for k in (2, 1, 0):
        run = qm[128 * k : 128 * k + 128] + send(run.astype(BF), along(-1)).astype(F32)
    return loss, run.astype(BF), passage_grad


def solution(mesh):
    return jax.shard_map(
        local,
        mesh=mesh,
        in_specs=(P(AXES, None), P(AXES, None), P(AXES), P(AXES, None), P(AXES, None)),
        out_specs=(P(AXES), P(AXES, None), P(AXES, None)),
        check_vma=False,
    )
```

```python
import jax
import jax.numpy as jnp
from jax import lax
from jax.experimental import pallas as pl
from jax.experimental.pallas import tpu as pltpu
from jax.sharding import PartitionSpec as P

AXES = ("group", "dp")
SHARP = 1.0 / 0.02
FLOOR = -1e30
BF = jnp.bfloat16
F32 = jnp.float32
WIDTH = 2048
VMEM = pl.BlockSpec(memory_space=pltpu.VMEM)
SMEM = pl.BlockSpec(memory_space=pltpu.SMEM)


def index(y, x, z, c):
    return (((y % 4) * 4 + x % 4) * 4 + z % 4) * 2 + c % 2


def pairs(step):
    found = []
    for y in range(4):
        for x in range(4):
            for z in range(4):
                for c in range(2):
                    found.append((index(y, x, z, c), index(*step(y, x, z, c))))
    return found


def first(d):
    return pairs(lambda y, x, z, c: (y, x, z + d, c) if c else (y, x + d, z, c))


def second(d):
    return pairs(lambda y, x, z, c: (y, x + d, z, c) if c else (y, x, z + d, c))


def along(d):
    return pairs(lambda y, x, z, c: (y - d, x, z, c) if c else (y + d, x, z, c))


CORE = pairs(lambda y, x, z, c: (y, x, z, 1 - c))


def send(v, perm):
    return lax.ppermute(v, AXES, perm)


def tied(*v):
    return lax.optimization_barrier(v)


def join(*v):
    return jnp.concatenate(v, axis=0)


def call(kernel, outs, specs, flops=0, nbytes=0, scratch=()):
    return pl.pallas_call(
        kernel,
        out_shape=outs,
        in_specs=specs,
        out_specs=jax.tree.map(lambda _: VMEM, outs),
        scratch_shapes=scratch,
        compiler_params=pltpu.CompilerParams(vmem_limit_bytes=32 * 2**20),
        cost_estimate=pl.CostEstimate(flops=flops, bytes_accessed=nbytes, transcendentals=0),
    )


def shape(r, c, t):
    return jax.ShapeDtypeStruct((r, c), t)


def pack_kernel(q_ref, owner_ref, row_ref, pos_ref, out_ref):
    out_ref[0:128, :] = q_ref[...]

    def turned(ref):
        wide = jnp.concatenate([ref[...], jnp.zeros((128, 112), jnp.int32)], axis=1).astype(F32)
        return jnp.transpose(wide)[0:16]

    pos = pos_ref[...]
    high = (pos // 64).astype(F32)
    low = (pos % 64).astype(F32)
    third = jnp.concatenate([high, low, jnp.zeros((14, 128), F32)], axis=0)
    meta = jnp.concatenate([turned(owner_ref), turned(row_ref), third], axis=1)
    out_ref[128:144, 0:384] = meta.astype(BF)
    out_ref[128:144, 384:WIDTH] = jnp.zeros((16, WIDTH - 384), BF)


def owner_id(place, piece, k1):
    x, z, core = place[1], place[2], place[3]
    kx = jnp.where(core == 0, k1, piece)
    kz = jnp.where(core == 0, piece, k1)
    return (lax.rem(x - kx + 4, 4) * 4 + lax.rem(z - kz + 4, 4)) * 2 + core


ORDER = {0: 0, 1: 1, 3: 2}
PIECES = (0, 1, 2, 3)


def steps(n):
    return lax.broadcasted_iota(jnp.int32, (64, n), 0).astype(F32) + 1.0


def score_block(place, piece, pair, a, b, raw, t_ref, write):
    rows = []
    owners = jnp.concatenate([a[128:144, 0:128], b[128:144, 0:128]], axis=1).astype(F32)
    spots = jnp.concatenate([a[128:144, 128:256], b[128:144, 128:256]], axis=1).astype(F32) + 1.0
    step = steps(256)
    hard, where = [], []
    for k1 in range(4):
        whole = (place[0] * 32 + owner_id(place, piece, k1)).astype(F32)
        spot = jnp.sum(jnp.where(owners == whole, spots, 0.0), axis=0, keepdims=True)
        part = raw[64 * k1 : 64 * k1 + 64]
        found = jnp.sum(jnp.where(step == spot, part, 0.0), axis=0, keepdims=True) * SHARP
        hard.append(jnp.where(spot > 0, found, FLOOR))
        where.append(spot)
    top = jnp.maximum(jnp.maximum(hard[0], hard[1]), jnp.maximum(hard[2], hard[3]))
    chosen = jnp.zeros((1, 256), F32)
    marks = [chosen] * 4
    total = chosen
    if pair == 0:
        scores = raw * SHARP
        top = jnp.maximum(top, jnp.max(scores, axis=0, keepdims=True))
        t = jnp.exp(scores - top)
        t_ref[...] = t
        total = jnp.sum(t, axis=0, keepdims=True)
        pos = jnp.concatenate([a[128:144, 256:384], b[128:144, 256:384]], axis=1).astype(F32)
        marks = []
        for k1 in range(4):
            mine = owner_id(place, piece, k1).astype(F32)
            mark = jnp.where(pos[0:1] == mine, pos[1:2] + 1.0, 0.0)
            part = scores[64 * k1 : 64 * k1 + 64]
            chosen = chosen + jnp.sum(jnp.where(step == mark, part, 0.0), axis=0, keepdims=True)
            marks.append(mark)
    for k1 in range(4):
        total = total + jnp.where(where[k1] > 0, jnp.exp(hard[k1] - top), 0.0)
    write(jnp.concatenate([*hard, *where, top, total, chosen, *marks, jnp.zeros((1, 256), F32)], axis=0))


def product(p, a, b):
    q = jnp.concatenate([a[0:128, :], b[0:128, :]], axis=0)
    return lax.dot_general(p, q, (((1,), (1,)), ((), ())), preferred_element_type=F32)


def writer(ref, rows, cols):
    def write(v):
        ref[rows : rows + 16, cols : cols + 256] = v

    return write


def early_kernel(place_ref, *refs):
    p_refs, q_refs, ts, info = refs[0:3], refs[3:9], refs[9:12], refs[12]
    place = [place_ref[i] for i in range(4)]
    p = jnp.concatenate([r[...] for r in p_refs], axis=0)
    for pair in range(3):
        a, b = q_refs[2 * pair], q_refs[2 * pair + 1]
        raw = product(p, a, b)
        for i, piece in enumerate((0, 1, 3)):
            score_block(
                place, piece, pair, a, b, raw[256 * i : 256 * i + 256], ts[i], writer(info, 16 * i, 256 * pair)
            )


class Info:
    def __init__(self, a, b, c):
        self.refs = a, b, c

    def rows(self, piece, pair, first, last):
        a, b, c = self.refs
        cols = slice(256 * pair, 256 * pair + 256)
        if piece == 2:
            return c[first:last, cols]
        i = 16 * ORDER[piece]
        if pair < 3:
            return a[i + first : i + last, cols]
        return b[i + first : i + last, 0:256]


def merge(a, b):
    top = jnp.maximum(a[0], b[0])
    total = a[1] * jnp.exp(a[0] - top) + b[1] * jnp.exp(b[0] - top)
    return top, total, a[2] + b[2]


def unpack(v):
    return v[0:1], v[1:2], v[2:3]


def late_kernel(place_ref, *refs):
    p_refs, low, high, q_refs, info_a = refs[0:3], refs[3], refs[4], refs[5:13], refs[13]
    t_ref, info_b, info_c, stats_ref = refs[14:]
    place = [place_ref[i] for i in range(4)]
    far = jnp.concatenate([low[...], high[...]], axis=0)
    for pair in range(4):
        a, b = q_refs[2 * pair], q_refs[2 * pair + 1]
        raw = product(far, a, b)
        score_block(place, 2, pair, a, b, raw, t_ref, writer(info_c, 0, 256 * pair))
    p = jnp.concatenate([r[...] for r in p_refs], axis=0)
    a, b = q_refs[6], q_refs[7]
    raw = product(p, a, b)
    for i, piece in enumerate((0, 1, 3)):
        score_block(place, piece, 3, a, b, raw[256 * i : 256 * i + 256], None, writer(info_b, 16 * i, 0))
    info = Info(info_a, info_b, info_c)
    for pair in range(4):
        acc = unpack(info.rows(0, pair, 8, 11))
        for piece in (1, 2, 3):
            acc = merge(acc, unpack(info.rows(piece, pair, 8, 11)))
        stats_ref[:, 256 * pair : 256 * pair + 256] = jnp.concatenate([*acc, jnp.zeros((5, 256), F32)], axis=0)


def query_kernel(half, *refs):
    ts, infos, stats, p_refs, out_ref, turned = refs[0:4], refs[4:7], refs[7], refs[8:13], refs[13], refs[14]
    info = Info(*infos)
    step = steps(128)
    side = slice(128 * half, 128 * half + 128)
    for piece in PIECES:
        cols = slice(256 * piece, 256 * piece + 256)
        for pair in range(4):
            top = stats[0:1, 256 * pair + 128 * half : 256 * pair + 128 * half + 128]
            rows = info.rows(piece, pair, 0, 16)[:, side]
            parts = []
            marks = []
            for k1 in range(4):
                part = jnp.where(step == rows[4 + k1 : 5 + k1], jnp.exp(rows[k1 : k1 + 1] - top), 0.0)
                if pair == 0:
                    t = ts[piece][64 * k1 : 64 * k1 + 64, side] * jnp.exp(rows[8:9] - top)
                    mark = step == rows[11 + k1 : 12 + k1]
                    part = part + jnp.where(mark, 0.0, t)
                    marks.append(jnp.where(mark, 1.0, 0.0))
                parts.append(part)
            turned[128 * pair : 128 * pair + 128, cols] = jnp.transpose(jnp.concatenate(parts, axis=0).astype(BF))
            if pair == 0:
                turned[512:640, cols] = jnp.transpose(jnp.concatenate(marks, axis=0).astype(BF))
    for n in range(4):
        cols = slice(512 * n, 512 * n + 512)
        p = jnp.concatenate([r[:, cols] for r in p_refs], axis=0)
        out_ref[:, cols] = jnp.dot(turned[...], p, preferred_element_type=F32).astype(out_ref.dtype)


def swap(v):
    return jnp.concatenate([v[:, 128 * (i ^ 1) : 128 * (i ^ 1) + 128] for i in range(8)], axis=1)


def total_kernel(raw, other, stats, g1, g2, g3, lse_ref, loss_ref, factor_ref):
    acc = unpack(stats[...])
    for t, got in ((1, g1), (2, g2), (3, g3)):
        v = got[...]
        picked = []
        for i in range(4):
            j, k = (i - t) % 4, (i + t) % 4
            picked += [v[:, 256 * j : 256 * j + 128], v[:, 256 * k + 128 : 256 * k + 256]]
        acc = merge(acc, unpack(jnp.concatenate(picked, axis=1)))
    lse = acc[0] + jnp.log(acc[1])
    lse_ref[...] = jnp.broadcast_to(lse, (8, 1024))
    chosen = acc[2][:, 0:128]
    loss_ref[...] = jnp.broadcast_to(lse[:, 0:128] - chosen, (8, 128))
    rows = []
    for top in (raw[0:1, :], swap(other[...])[0:1]):
        f = jnp.exp(top - lse) * SHARP
        rows += [f[:, 256 * j : 256 * j + 128] for j in range(4)]
    pos = ((jnp.exp(chosen - lse[:, 0:128]) - 1.0) * SHARP).astype(BF).astype(F32)
    factor_ref[...] = jnp.transpose(jnp.concatenate([*rows, pos, jnp.zeros((119, 128), F32)], axis=0))


def coefficients(info, piece, t_ref, lse_ref, c_ref, at):
    step = steps(256)
    for pair in range(4):
        cols = slice(256 * pair, 256 * pair + 256)
        lse = lse_ref[0:1, cols]
        rows = info.rows(piece, pair, 0, 16)
        parts = []
        for k1 in range(4):
            part = jnp.where(step == rows[4 + k1 : 5 + k1], jnp.exp(rows[k1 : k1 + 1] - lse) * SHARP, 0.0)
            if pair == 0:
                t = t_ref[64 * k1 : 64 * k1 + 64, :] * jnp.exp(rows[8:9] - lse)
                t = t - jnp.where(step == rows[11 + k1 : 12 + k1], 1.0, 0.0)
                part = part + t * SHARP
            parts.append(part)
        c_ref[at : at + 256, cols] = jnp.concatenate(parts, axis=0).astype(BF)


def far_kernel(t_ref, *refs):
    infos, lse_ref, q_refs = refs[0:3], refs[3], refs[4:12]
    low_ref, high_ref, c = refs[12:]
    coefficients(Info(*infos), 2, t_ref, lse_ref, c, 0)
    for n in range(4):
        cols = slice(512 * n, 512 * n + 512)
        q = jnp.concatenate([r[0:128, cols] for r in q_refs], axis=0)
        g = jnp.dot(c[...], q, preferred_element_type=F32).astype(BF)
        low_ref[:, cols] = g[0:128]
        high_ref[:, cols] = g[128:256]


def near_kernel(*refs):
    ts, infos, lse_ref, q_refs = refs[0:3], refs[3:6], refs[6], refs[7:15]
    zero, one_low, one_high, three_low, three_high, c = refs[15:]
    info = Info(*infos)
    for i, piece in enumerate((0, 1, 3)):
        coefficients(info, piece, ts[i], lse_ref, c, 256 * i)
    for n in range(4):
        cols = slice(512 * n, 512 * n + 512)
        q = jnp.concatenate([r[0:128, cols] for r in q_refs], axis=0)
        g = jnp.dot(c[...], q, preferred_element_type=F32)
        zero[:, cols] = g[0:256]
        one_low[:, cols] = g[256:384]
        one_high[:, cols] = g[384:512].astype(BF)
        three_low[:, cols] = g[512:640].astype(BF)
        three_high[:, cols] = g[640:768]


def local(question_vectors, passages, positive, hard_owner, hard_row):
    group = lax.axis_index("group")
    dp = lax.axis_index("dp")
    place = jnp.stack([group, dp // 8, dp // 2 % 4, dp % 2]).astype(jnp.int32)

    packed = call(pack_kernel, shape(144, WIDTH, BF), [VMEM] * 4)(
        question_vectors, hard_owner, hard_row, positive.reshape(1, 128)
    )

    back = send(passages, first(1))
    ahead = send(passages, first(-1))
    across = send(passages, first(2))
    q1 = send(packed, along(1))
    s0 = send(packed, CORE)
    back, ahead, across, q1 = tied(back, ahead, across, q1)
    plane = join(passages, back, across, ahead)
    up = send(plane, second(1))
    down = send(plane, second(-1))
    q2 = send(q1, along(1))
    s1 = send(q1, CORE)
    up, down, q2 = tied(up, down, q2)
    low = send(up[:128], second(1))
    high = send(down[128:], second(-1))
    q3 = send(q2, along(1))
    s2 = send(q2, CORE)
    low, high, q3 = tied(low, high, q3)
    s3 = send(q3, CORE)
    tiles = (packed, s0, q1, s1, q2, s2, q3, s3)

    t0, t1, t3, info_a = call(
        early_kernel,
        (shape(256, 256, F32), shape(256, 256, F32), shape(256, 256, F32), shape(48, 768, F32)),
        [SMEM] + [VMEM] * 9,
        2 * 768 * 768 * WIDTH,
    )(place, plane, up, down, *tiles[:6])
    t2, info_b, info_c, raw = call(
        late_kernel,
        (shape(256, 256, F32), shape(48, 256, F32), shape(16, 1024, F32), shape(8, 1024, F32)),
        [SMEM] + [VMEM] * 14,
        2 * 448 * 1024 * WIDTH,
    )(place, plane, up, down, low, high, *tiles, info_a)

    other = send(raw, CORE)
    stats = jnp.concatenate([*merge(unpack(raw), unpack(swap(other))), jnp.zeros((5, 1024), F32)], axis=0)
    g1 = send(stats, along(1))
    g2 = send(stats, along(2))
    g3 = send(stats, along(3))
    infos = (info_a, info_b, info_c)
    operands = (t0, t1, t2, t3, *infos, raw, plane, up, low, high, down)

    def query(half, kind):
        return call(
            lambda *r: query_kernel(half, *r),
            shape(640, WIDTH, kind),
            [VMEM] * 13,
            2 * 640 * 1024 * WIDTH,
            scratch=[pltpu.VMEM((640, 1024), BF)],
        )(*operands)

    theirs = send(query(1, BF), CORE)
    mine = query(0, F32)
    lse, loss, factor = call(
        total_kernel, (shape(8, 1024, F32), shape(8, 128, F32), shape(128, 128, F32)), [VMEM] * 6
    )(raw, other, stats, g1, g2, g3)

    two_low, two_high = call(
        far_kernel,
        (shape(128, WIDTH, BF), shape(128, WIDTH, BF)),
        [VMEM] * 13,
        2 * 256 * 1024 * WIDTH,
        scratch=[pltpu.VMEM((256, 1024), BF)],
    )(t2, *infos, lse, *tiles)
    from_high = send(two_low, second(-1))
    from_low = send(two_high, second(1))

    def block(k):
        a = mine[128 * k : 128 * k + 128] * factor[:, k : k + 1]
        return a + theirs[128 * k : 128 * k + 128].astype(F32) * factor[:, 4 + k : 5 + k]

    run = block(3)
    for k in (2, 1, 0):
        run = block(k) + send(run.astype(BF), along(-1)).astype(F32)
    query_grad = run + (mine[512:640] + theirs[512:640].astype(F32)) * factor[:, 8:9]

    zero, one_low, one_high, three_low, three_high = call(
        near_kernel,
        (
            shape(256, WIDTH, F32),
            shape(128, WIDTH, F32),
            shape(128, WIDTH, BF),
            shape(128, WIDTH, BF),
            shape(128, WIDTH, F32),
        ),
        [VMEM] * 15,
        2 * 768 * 1024 * WIDTH,
        scratch=[pltpu.VMEM((768, 1024), BF)],
    )(t0, t1, t3, *infos, lse, *tiles)
    r1b = send(one_high, second(-1))
    r3a = send(three_low, second(1))
    r1a = send((one_low + from_high.astype(F32)).astype(BF), second(-1))
    r3b = send((three_high + from_low.astype(F32)).astype(BF), second(1))
    g = zero + (join(r1a.astype(F32), r1b.astype(F32)) + join(r3a.astype(F32), r3b.astype(F32)))
    passage_grad = g[0:64]
    for k, d in ((2, 2), (1, -1), (3, 1)):
        passage_grad = passage_grad + send(g[64 * k : 64 * k + 64].astype(BF), first(d)).astype(F32)
    return loss[0], query_grad.astype(BF), passage_grad.astype(BF)


def solution(mesh):
    return jax.shard_map(
        local,
        mesh=mesh,
        in_specs=(P(AXES, None), P(AXES, None), P(AXES), P(AXES, None), P(AXES, None)),
        out_specs=(P(AXES), P(AXES, None), P(AXES, None)),
        check_vma=False,
    )
```

```python
import jax
import jax.numpy as jnp
from jax import lax
from jax.experimental import pallas as pl
from jax.experimental.pallas import tpu as pltpu
from jax.sharding import PartitionSpec as P

AXES = ("group", "dp")
SHARP = 1.0 / 0.02
FLOOR = -1e30
BF = jnp.bfloat16
F32 = jnp.float32
WIDTH = 2048
VMEM = pl.BlockSpec(memory_space=pltpu.VMEM)
ANY = pl.BlockSpec(memory_space=pl.ANY)


def index(y, x, z, c):
    return (((y % 4) * 4 + x % 4) * 4 + z % 4) * 2 + c % 2


def pairs(step):
    found = []
    for y in range(4):
        for x in range(4):
            for z in range(4):
                for c in range(2):
                    found.append((index(y, x, z, c), index(*step(y, x, z, c))))
    return found


def first(d):
    return pairs(lambda y, x, z, c: (y, x, z + d, c) if c else (y, x + d, z, c))


def second(d):
    return pairs(lambda y, x, z, c: (y, x + d, z, c) if c else (y, x, z + d, c))


def along(d):
    return pairs(lambda y, x, z, c: (y - d, x, z, c) if c else (y + d, x, z, c))


CORE = pairs(lambda y, x, z, c: (y, x, z, 1 - c))


def send(v, perm):
    return lax.ppermute(v, AXES, perm)


def tied(*v):
    return lax.optimization_barrier(v)


def join(*v):
    return jnp.concatenate(v, axis=0)


def call(kernel, outs, specs, flops=0, nbytes=0, scratch=(), limit=16):
    return pl.pallas_call(
        kernel,
        out_shape=outs,
        in_specs=specs,
        out_specs=jax.tree.map(lambda _: VMEM, outs),
        scratch_shapes=scratch,
        compiler_params=pltpu.CompilerParams(vmem_limit_bytes=limit * 2**20),
        cost_estimate=pl.CostEstimate(flops=flops, bytes_accessed=nbytes, transcendentals=0),
    )


def shape(r, c, t):
    return jax.ShapeDtypeStruct((r, c), t)


def pack_kernel(q_ref, owner_ref, row_ref, pos_ref, p_ref, out_ref, kept_ref, owner, row, pos, sems):
    copies = []
    for i, (src, dst) in enumerate(
        ((owner_ref, owner), (row_ref, row), (pos_ref, pos), (q_ref, out_ref.at[0:128, :]), (p_ref, kept_ref))
    ):
        copies.append(pltpu.make_async_copy(src, dst, sems.at[i]))
        copies[-1].start()
    out_ref[128:144, 384:WIDTH] = jnp.zeros((16, WIDTH - 384), BF)
    for c in copies[:3]:
        c.wait()
    high = (pos[...] // 64).astype(F32)
    low = (pos[...] % 64).astype(F32)
    third = jnp.concatenate([high, low, jnp.zeros((14, 128), F32)], axis=0)
    meta = jnp.concatenate([owner[...].astype(F32), row[...].astype(F32), third], axis=1)
    out_ref[128:144, 0:384] = meta.astype(BF)
    copies[3].wait()
    copies[4].wait()


def join_kernel(*refs):
    for i, r in enumerate(refs[:4]):
        refs[4][64 * i : 64 * i + 64, :] = r[...]


def whereabouts():
    dp = lax.axis_index("dp")
    return lax.axis_index("group"), dp // 8, lax.rem(dp // 2, 4), lax.rem(dp, 2)


def owner_id(place, piece, k1):
    x, z, core = place[1], place[2], place[3]
    kx = jnp.where(core == 0, k1, piece)
    kz = jnp.where(core == 0, piece, k1)
    return (lax.rem(x - kx + 4, 4) * 4 + lax.rem(z - kz + 4, 4)) * 2 + core


PIECES = (0, 1, 2, 3)


def steps(n):
    return lax.broadcasted_iota(jnp.int32, (64, n), 0).astype(F32) + 1.0


def score_block(place, piece, pair, a, b, raw, t_ref, write):
    rows = []
    owners = jnp.concatenate([a[128:144, 0:128], b[128:144, 0:128]], axis=1).astype(F32)
    spots = jnp.concatenate([a[128:144, 128:256], b[128:144, 128:256]], axis=1).astype(F32) + 1.0
    step = steps(256)
    hard, where = [], []
    for k1 in range(4):
        whole = (place[0] * 32 + owner_id(place, piece, k1)).astype(F32)
        spot = jnp.sum(jnp.where(owners == whole, spots, 0.0), axis=0, keepdims=True)
        part = raw[64 * k1 : 64 * k1 + 64]
        found = jnp.sum(jnp.where(step == spot, part, 0.0), axis=0, keepdims=True) * SHARP
        hard.append(jnp.where(spot > 0, found, FLOOR))
        where.append(spot)
    top = jnp.maximum(jnp.maximum(hard[0], hard[1]), jnp.maximum(hard[2], hard[3]))
    chosen = jnp.zeros((1, 256), F32)
    marks = [chosen] * 4
    total = chosen
    if pair == 0:
        scores = raw * SHARP
        top = jnp.maximum(top, jnp.max(scores, axis=0, keepdims=True))
        t = jnp.exp(scores - top)
        t_ref[...] = t
        total = jnp.sum(t, axis=0, keepdims=True)
        pos = jnp.concatenate([a[128:144, 256:384], b[128:144, 256:384]], axis=1).astype(F32)
        marks = []
        for k1 in range(4):
            mine = owner_id(place, piece, k1).astype(F32)
            mark = jnp.where(pos[0:1] == mine, pos[1:2] + 1.0, 0.0)
            part = scores[64 * k1 : 64 * k1 + 64]
            chosen = chosen + jnp.sum(jnp.where(step == mark, part, 0.0), axis=0, keepdims=True)
            marks.append(mark)
    for k1 in range(4):
        total = total + jnp.where(where[k1] > 0, jnp.exp(hard[k1] - top), 0.0)
    write(jnp.concatenate([*hard, *where, top, total, chosen, *marks, jnp.zeros((1, 256), F32)], axis=0))


def product(p, a, b):
    q = jnp.concatenate([a[0:128, :], b[0:128, :]], axis=0)
    return lax.dot_general(p, q, (((1,), (1,)), ((), ())), preferred_element_type=F32)


def writer(ref, rows, cols):
    def write(v):
        ref[rows : rows + 16, cols : cols + 256] = v

    return write


def early_kernel(*refs):
    p_refs, q_refs, ts, info = refs[0:4], refs[4:10], refs[10:14], refs[14]
    place = whereabouts()
    p = jnp.concatenate([r[...] for r in p_refs], axis=0)
    for pair in range(3):
        a, b = q_refs[2 * pair], q_refs[2 * pair + 1]
        raw = product(p, a, b)
        for i in PIECES:
            part = raw[256 * i : 256 * i + 256]
            score_block(place, i, pair, a, b, part, ts[i], writer(info, 16 * i, 256 * pair))


class Info:
    def __init__(self, a, b):
        self.refs = a, b

    def rows(self, piece, pair, first, last):
        a, b = self.refs
        i = 16 * piece
        if pair < 3:
            return a[i + first : i + last, 256 * pair : 256 * pair + 256]
        return b[i + first : i + last, 0:256]


def merge(a, b):
    top = jnp.maximum(a[0], b[0])
    total = a[1] * jnp.exp(a[0] - top) + b[1] * jnp.exp(b[0] - top)
    return top, total, a[2] + b[2]


def unpack(v):
    return v[0:1], v[1:2], v[2:3]


def late_kernel(*refs):
    p_refs, q_refs, info_a, info_b, stats_ref = refs[0:4], refs[4:6], refs[6], refs[7], refs[8]
    place = whereabouts()
    p = jnp.concatenate([r[...] for r in p_refs], axis=0)
    raw = product(p, q_refs[0], q_refs[1])
    for i in PIECES:
        part = raw[256 * i : 256 * i + 256]
        score_block(place, i, 3, q_refs[0], q_refs[1], part, None, writer(info_b, 16 * i, 0))
    info = Info(info_a, info_b)
    for pair in range(4):
        acc = unpack(info.rows(0, pair, 8, 11))
        for piece in (1, 2, 3):
            acc = merge(acc, unpack(info.rows(piece, pair, 8, 11)))
        stats_ref[:, 256 * pair : 256 * pair + 256] = jnp.concatenate([*acc, jnp.zeros((5, 256), F32)], axis=0)


def query_kernel(half, *refs):
    ts, infos, stats, p_refs, out_ref, turned = refs[0:4], refs[4:6], refs[6], refs[7:11], refs[12], refs[13]
    info = Info(*infos)
    step = steps(128)
    side = slice(128 * half, 128 * half + 128)
    for piece in PIECES:
        cols = slice(256 * piece, 256 * piece + 256)
        for pair in range(4):
            top = stats[0:1, 256 * pair + 128 * half : 256 * pair + 128 * half + 128]
            rows = info.rows(piece, pair, 0, 16)[:, side]
            parts = []
            marks = []
            for k1 in range(4):
                part = jnp.where(step == rows[4 + k1 : 5 + k1], jnp.exp(rows[k1 : k1 + 1] - top), 0.0)
                if pair == 0:
                    t = ts[piece][64 * k1 : 64 * k1 + 64, side] * jnp.exp(rows[8:9] - top)
                    mark = step == rows[11 + k1 : 12 + k1]
                    part = part + jnp.where(mark, 0.0, t)
                    marks.append(jnp.where(mark, 1.0, 0.0))
                parts.append(part)
            turned[128 * pair : 128 * pair + 128, cols] = jnp.transpose(jnp.concatenate(parts, axis=0).astype(BF))
            if pair == 0:
                turned[512:640, cols] = jnp.transpose(jnp.concatenate(marks, axis=0).astype(BF))
    for n in range(4):
        cols = slice(512 * n, 512 * n + 512)
        p = jnp.concatenate([r[:, cols] for r in p_refs], axis=0)
        out_ref[:, cols] = jnp.dot(turned[...], p, preferred_element_type=F32).astype(out_ref.dtype)


def swap(v):
    return jnp.concatenate([v[:, 128 * (i ^ 1) : 128 * (i ^ 1) + 128] for i in range(8)], axis=1)


def merge_kernel(raw, other, out_ref):
    both = merge(unpack(raw[...]), unpack(swap(other[...])))
    out_ref[...] = jnp.concatenate([*both, jnp.zeros((5, 1024), F32)], axis=0)


def block_kernel(k, mine, theirs, factor, *refs):
    out_ref = refs[-1]
    rows = slice(128 * k, 128 * k + 128)
    f = factor[...]
    for n in range(4):
        cols = slice(512 * n, 512 * n + 512)
        v = mine[rows, cols] * f[:, k : k + 1] + theirs[rows, cols].astype(F32) * f[:, 4 + k : 5 + k]
        if k == 0:
            v = v + (mine[512:640, cols] + theirs[512:640, cols].astype(F32)) * f[:, 8:9]
        if k < 3:
            v = v + refs[0][:, cols].astype(F32)
        out_ref[:, cols] = v.astype(BF)


def gather_kernel(zero, one, two, three, *outs):
    for k in range(4):
        rows = slice(64 * k, 64 * k + 64)
        v = zero[rows] + two[rows].astype(F32) + (one[rows].astype(F32) + three[rows].astype(F32))
        outs[k][...] = v.astype(outs[k].dtype)


def last_kernel(a, b, c, d, _, out_ref):
    v = a[...] + c[...].astype(F32) + (b[...].astype(F32) + d[...].astype(F32))
    out_ref[...] = v.astype(BF)


def total_kernel(raw, other, stats, g1, g2, g3, lse_ref, loss_ref, factor_ref):
    acc = unpack(stats[...])
    for t, got in ((1, g1), (2, g2), (3, g3)):
        v = got[...]
        picked = []
        for i in range(4):
            j, k = (i - t) % 4, (i + t) % 4
            picked += [v[:, 256 * j : 256 * j + 128], v[:, 256 * k + 128 : 256 * k + 256]]
        acc = merge(acc, unpack(jnp.concatenate(picked, axis=1)))
    lse = acc[0] + jnp.log(acc[1])
    lse_ref[...] = jnp.broadcast_to(lse, (8, 1024))
    chosen = acc[2][:, 0:128]
    loss_ref[...] = jnp.broadcast_to(lse[:, 0:128] - chosen, (8, 128))
    rows = []
    for top in (raw[0:1, :], swap(other[...])[0:1]):
        f = jnp.exp(top - lse) * SHARP
        rows += [f[:, 256 * j : 256 * j + 128] for j in range(4)]
    pos = ((jnp.exp(chosen - lse[:, 0:128]) - 1.0) * SHARP).astype(BF).astype(F32)
    factor_ref[...] = jnp.transpose(jnp.concatenate([*rows, pos, jnp.zeros((119, 128), F32)], axis=0))


def coefficients(info, piece, t_ref, lse_ref, c_ref, at):
    step = steps(256)
    for pair in range(4):
        cols = slice(256 * pair, 256 * pair + 256)
        lse = lse_ref[0:1, cols]
        rows = info.rows(piece, pair, 0, 16)
        parts = []
        for k1 in range(4):
            part = jnp.where(step == rows[4 + k1 : 5 + k1], jnp.exp(rows[k1 : k1 + 1] - lse) * SHARP, 0.0)
            if pair == 0:
                t = t_ref[64 * k1 : 64 * k1 + 64, :] * jnp.exp(rows[8:9] - lse)
                t = t - jnp.where(step == rows[11 + k1 : 12 + k1], 1.0, 0.0)
                part = part + t * SHARP
            parts.append(part)
        c_ref[at : at + 256, cols] = jnp.concatenate(parts, axis=0).astype(BF)


def far_kernel(t_ref, *refs):
    infos, lse_ref, q_refs = refs[0:2], refs[2], refs[3:11]
    out_ref, c = refs[11:]
    coefficients(Info(*infos), 2, t_ref, lse_ref, c, 0)
    for n in range(4):
        cols = slice(512 * n, 512 * n + 512)
        q = jnp.concatenate([r[0:128, cols] for r in q_refs], axis=0)
        out_ref[:, cols] = jnp.dot(c[...], q, preferred_element_type=F32).astype(BF)


def near_kernel(*refs):
    ts, infos, lse_ref, q_refs = refs[0:3], refs[3:5], refs[5], refs[6:14]
    zero, one, three, c = refs[15:]
    info = Info(*infos)
    for i, piece in enumerate((0, 1, 3)):
        coefficients(info, piece, ts[i], lse_ref, c, 256 * i)
    for n in range(4):
        cols = slice(512 * n, 512 * n + 512)
        q = jnp.concatenate([r[0:128, cols] for r in q_refs], axis=0)
        g = jnp.dot(c[...], q, preferred_element_type=F32)
        zero[:, cols] = g[0:256]
        one[:, cols] = g[256:512].astype(BF)
        three[:, cols] = g[512:768].astype(BF)


def local(question_vectors, passages, positive, hard_owner, hard_row):
    packed, kept = call(
        pack_kernel,
        (shape(144, WIDTH, BF), shape(64, WIDTH, BF)),
        [ANY] * 5,
        scratch=[
            pltpu.VMEM((16, 128), jnp.int32),
            pltpu.VMEM((16, 128), jnp.int32),
            pltpu.VMEM((1, 128), jnp.int32),
            pltpu.SemaphoreType.DMA((5,)),
        ],
        limit=56,
    )(question_vectors, hard_owner.T, hard_row.T, positive.reshape(1, 128), passages)

    back = send(passages, first(1))
    ahead = send(passages, first(-1))
    across = send(passages, first(2))
    q1 = send(packed, along(1))
    s0 = send(packed, CORE)
    back, ahead, across, q1, s0 = tied(back, ahead, across, q1, s0)
    plane = call(join_kernel, shape(256, WIDTH, BF), [VMEM] * 4)(kept, back, across, ahead)
    up = send(plane, second(1))
    down = send(plane, second(-1))
    over = send(plane, second(2))
    q2 = send(q1, along(1))
    s1 = send(q1, CORE)
    q3 = send(q2, along(1))
    s2 = send(q2, CORE)
    s3 = send(q3, CORE)
    tiles = (packed, s0, q1, s1, q2, s2, q3, s3)

    pieces = (plane, up, over, down)
    tile = shape(256, 256, F32)
    t0, t1, t2, t3, info_a = call(
        early_kernel, (tile, tile, tile, tile, shape(64, 768, F32)), [VMEM] * 10, 2 * 1024 * 768 * WIDTH
    )(*pieces, *tiles[:6])
    info_b, raw = call(
        late_kernel, (shape(64, 256, F32), shape(8, 1024, F32)), [VMEM] * 7, 2 * 1024 * 256 * WIDTH
    )(*pieces, *tiles[6:], info_a)

    other = send(raw, CORE)
    stats = call(merge_kernel, shape(8, 1024, F32), [VMEM] * 2)(raw, other)
    g1 = send(stats, along(1))
    g2 = send(stats, along(2))
    g3 = send(stats, along(3))
    infos = (info_a, info_b)
    operands = (t0, t1, t2, t3, *infos, raw, *pieces, stats)

    def query(half, kind):
        return call(
            lambda *r: query_kernel(half, *r),
            shape(640, WIDTH, kind),
            [VMEM] * 12,
            2 * 640 * 1024 * WIDTH,
            scratch=[pltpu.VMEM((640, 1024), BF)],
        )(*operands)

    theirs = send(query(1, BF), CORE)
    mine = query(0, F32)
    lse, loss, factor = call(
        total_kernel, (shape(8, 1024, F32), shape(8, 128, F32), shape(128, 128, F32)), [VMEM] * 6
    )(raw, other, stats, g1, g2, g3)

    far = call(far_kernel, shape(256, WIDTH, BF), [VMEM] * 12, 2 * 256 * 1024 * WIDTH, scratch=[pltpu.VMEM((256, 1024), BF)])(
        t2, *infos, lse, *tiles
    )
    two = send(far, second(2))

    def block(k, *got):
        kernel = lambda *r: block_kernel(k, *r)
        return call(kernel, shape(128, WIDTH, BF), [VMEM] * (3 + len(got)))(mine, theirs, factor, *got)

    run = block(3)
    for k in (2, 1, 0):
        run = block(k, send(run, along(-1)))

    zero, one, three = call(
        near_kernel,
        (shape(256, WIDTH, F32), shape(256, WIDTH, BF), shape(256, WIDTH, BF)),
        [VMEM] * 15,
        2 * 768 * 1024 * WIDTH,
        scratch=[pltpu.VMEM((768, 1024), BF)],
    )(t0, t1, t3, *infos, lse, *tiles, far)
    one = send(one, second(-1))
    three = send(three, second(1))
    half = shape(64, WIDTH, BF)
    g0, g1, g2, g3 = call(gather_kernel, (shape(64, WIDTH, F32), half, half, half), [VMEM] * 4)(zero, one, two, three)
    g2 = send(g2, first(2))
    g1 = send(g1, first(-1))
    g3 = send(g3, first(1))
    passage_grad = call(last_kernel, half, [VMEM] * 5)(g0, g1, g2, g3, run)
    return loss[0], run, passage_grad


def solution(mesh):
    return jax.shard_map(
        local,
        mesh=mesh,
        in_specs=(P(AXES, None), P(AXES, None), P(AXES), P(AXES, None), P(AXES, None)),
        out_specs=(P(AXES), P(AXES, None), P(AXES, None)),
        check_vma=False,
    )
```

```python
import jax
import jax.numpy as jnp
from jax import lax
from jax.experimental import pallas as pl
from jax.experimental.pallas import tpu as pltpu
from jax.sharding import PartitionSpec as P

AXES = ("group", "dp")
SHARP = 1.0 / 0.02
FLOOR = -1e30
BF = jnp.bfloat16
F32 = jnp.float32
WIDTH = 2048
VMEM = pl.BlockSpec(memory_space=pltpu.VMEM)
ANY = pl.BlockSpec(memory_space=pl.ANY)


def index(y, x, z, c):
    return (((y % 4) * 4 + x % 4) * 4 + z % 4) * 2 + c % 2


def pairs(step):
    found = []
    for y in range(4):
        for x in range(4):
            for z in range(4):
                for c in range(2):
                    found.append((index(y, x, z, c), index(*step(y, x, z, c))))
    return found


def first(d):
    return pairs(lambda y, x, z, c: (y, x, z + d, c) if c else (y, x + d, z, c))


def second(d):
    return pairs(lambda y, x, z, c: (y, x + d, z, c) if c else (y, x, z + d, c))


def along(d):
    return pairs(lambda y, x, z, c: (y - d, x, z, c) if c else (y + d, x, z, c))


CORE = pairs(lambda y, x, z, c: (y, x, z, 1 - c))


def send(v, perm):
    return lax.ppermute(v, AXES, perm)


def tied(*v):
    return lax.optimization_barrier(v)


def join(*v):
    return jnp.concatenate(v, axis=0)


def call(kernel, outs, specs, flops=0, nbytes=0, scratch=(), limit=16):
    return pl.pallas_call(
        kernel,
        out_shape=outs,
        in_specs=specs,
        out_specs=jax.tree.map(lambda _: VMEM, outs),
        scratch_shapes=scratch,
        compiler_params=pltpu.CompilerParams(vmem_limit_bytes=limit * 2**20),
        cost_estimate=pl.CostEstimate(flops=flops, bytes_accessed=nbytes, transcendentals=0),
    )


def shape(r, c, t):
    return jax.ShapeDtypeStruct((r, c), t)


def pack_kernel(q_ref, owner_ref, row_ref, pos_ref, out_ref, owner, row, pos, sems):
    copies = []
    for i, (src, dst) in enumerate(
        ((owner_ref, owner), (row_ref, row), (pos_ref, pos), (q_ref, out_ref.at[0:128, :]))
    ):
        copies.append(pltpu.make_async_copy(src, dst, sems.at[i]))
        copies[-1].start()
    out_ref[128:144, 384:WIDTH] = jnp.zeros((16, WIDTH - 384), BF)
    for c in copies[:3]:
        c.wait()
    high = (pos[...] // 64).astype(F32)
    low = (pos[...] % 64).astype(F32)
    third = jnp.concatenate([high, low, jnp.zeros((14, 128), F32)], axis=0)
    meta = jnp.concatenate([owner[...].astype(F32), row[...].astype(F32), third], axis=1)
    out_ref[128:144, 0:384] = meta.astype(BF)
    copies[3].wait()


def stage_kernel(a_ref, b_ref, a_out, b_out, sems):
    one = pltpu.make_async_copy(a_ref, a_out, sems.at[0])
    two = pltpu.make_async_copy(b_ref, b_out, sems.at[1])
    one.start()
    two.start()
    one.wait()
    two.wait()


def join_kernel(*refs):
    for i, r in enumerate(refs[:4]):
        refs[4][64 * i : 64 * i + 64, :] = r[...]


def whereabouts():
    dp = lax.axis_index("dp")
    return lax.axis_index("group"), dp // 8, lax.rem(dp // 2, 4), lax.rem(dp, 2)


def owner_id(place, piece, k1):
    x, z, core = place[1], place[2], place[3]
    kx = jnp.where(core == 0, k1, piece)
    kz = jnp.where(core == 0, piece, k1)
    return (lax.rem(x - kx + 4, 4) * 4 + lax.rem(z - kz + 4, 4)) * 2 + core


PIECES = (0, 1, 2, 3)


def steps(n):
    return lax.broadcasted_iota(jnp.int32, (64, n), 0).astype(F32) + 1.0


def score_block(place, piece, pair, a, b, raw, t_ref, write):
    rows = []
    owners = jnp.concatenate([a[128:144, 0:128], b[128:144, 0:128]], axis=1).astype(F32)
    spots = jnp.concatenate([a[128:144, 128:256], b[128:144, 128:256]], axis=1).astype(F32) + 1.0
    step = steps(256)
    hard, where = [], []
    for k1 in range(4):
        whole = (place[0] * 32 + owner_id(place, piece, k1)).astype(F32)
        spot = jnp.sum(jnp.where(owners == whole, spots, 0.0), axis=0, keepdims=True)
        part = raw[64 * k1 : 64 * k1 + 64]
        found = jnp.sum(jnp.where(step == spot, part, 0.0), axis=0, keepdims=True) * SHARP
        hard.append(jnp.where(spot > 0, found, FLOOR))
        where.append(spot)
    top = jnp.maximum(jnp.maximum(hard[0], hard[1]), jnp.maximum(hard[2], hard[3]))
    chosen = jnp.zeros((1, 256), F32)
    marks = [chosen] * 4
    total = chosen
    if pair == 0:
        scores = raw * SHARP
        top = jnp.maximum(top, jnp.max(scores, axis=0, keepdims=True))
        t = jnp.exp(scores - top)
        t_ref[...] = t
        total = jnp.sum(t, axis=0, keepdims=True)
        pos = jnp.concatenate([a[128:144, 256:384], b[128:144, 256:384]], axis=1).astype(F32)
        marks = []
        for k1 in range(4):
            mine = owner_id(place, piece, k1).astype(F32)
            mark = jnp.where(pos[0:1] == mine, pos[1:2] + 1.0, 0.0)
            part = scores[64 * k1 : 64 * k1 + 64]
            chosen = chosen + jnp.sum(jnp.where(step == mark, part, 0.0), axis=0, keepdims=True)
            marks.append(mark)
    for k1 in range(4):
        total = total + jnp.where(where[k1] > 0, jnp.exp(hard[k1] - top), 0.0)
    write(jnp.concatenate([*hard, *where, top, total, chosen, *marks, jnp.zeros((1, 256), F32)], axis=0))


def product(p, a, b):
    q = jnp.concatenate([a[0:128, :], b[0:128, :]], axis=0)
    return lax.dot_general(p, q, (((1,), (1,)), ((), ())), preferred_element_type=F32)


def writer(ref, rows, cols):
    def write(v):
        ref[rows : rows + 16, cols : cols + 256] = v

    return write


def early_kernel(pieces, *refs):
    p_refs, q_refs, ts, info = refs[0:2], refs[2:8], refs[8:10], refs[10]
    place = whereabouts()
    p = jnp.concatenate([r[...] for r in p_refs], axis=0)
    for pair in range(3):
        a, b = q_refs[2 * pair], q_refs[2 * pair + 1]
        raw = product(p, a, b)
        for i, piece in enumerate(pieces):
            part = raw[256 * i : 256 * i + 256]
            score_block(place, piece, pair, a, b, part, ts[i], writer(info, 16 * i, 256 * pair))


SOON, LATER = (0, 3), (1, 2)


class Info:
    def __init__(self, *refs):
        self.refs = refs

    def rows(self, piece, pair, first, last):
        if pair < 3:
            ref = self.refs[0 if piece in SOON else 1]
            i = 16 * (SOON if piece in SOON else LATER).index(piece)
            return ref[i + first : i + last, 256 * pair : 256 * pair + 256]
        i = 16 * piece
        return self.refs[2][i + first : i + last, 0:256]


def merge(a, b):
    top = jnp.maximum(a[0], b[0])
    total = a[1] * jnp.exp(a[0] - top) + b[1] * jnp.exp(b[0] - top)
    return top, total, a[2] + b[2]


def unpack(v):
    return v[0:1], v[1:2], v[2:3]


def late_kernel(*refs):
    p_refs, q_refs, soon, later, info_b, stats_ref = refs[0:4], refs[4:6], *refs[6:10]
    place = whereabouts()
    p = jnp.concatenate([r[...] for r in p_refs], axis=0)
    raw = product(p, q_refs[0], q_refs[1])
    for i in PIECES:
        part = raw[256 * i : 256 * i + 256]
        score_block(place, i, 3, q_refs[0], q_refs[1], part, None, writer(info_b, 16 * i, 0))
    info = Info(soon, later, info_b)
    for pair in range(4):
        acc = unpack(info.rows(0, pair, 8, 11))
        for piece in (1, 2, 3):
            acc = merge(acc, unpack(info.rows(piece, pair, 8, 11)))
        stats_ref[:, 256 * pair : 256 * pair + 256] = jnp.concatenate([*acc, jnp.zeros((5, 256), F32)], axis=0)


def query_kernel(half, *refs):
    ts, infos, stats, p_refs, out_ref, turned = refs[0:4], refs[4:7], refs[7], refs[8:12], refs[13], refs[14]
    info = Info(*infos)
    step = steps(128)
    side = slice(128 * half, 128 * half + 128)
    for piece in PIECES:
        cols = slice(256 * piece, 256 * piece + 256)
        for pair in range(4):
            top = stats[0:1, 256 * pair + 128 * half : 256 * pair + 128 * half + 128]
            rows = info.rows(piece, pair, 0, 16)[:, side]
            parts = []
            marks = []
            for k1 in range(4):
                part = jnp.where(step == rows[4 + k1 : 5 + k1], jnp.exp(rows[k1 : k1 + 1] - top), 0.0)
                if pair == 0:
                    t = ts[piece][64 * k1 : 64 * k1 + 64, side] * jnp.exp(rows[8:9] - top)
                    mark = step == rows[11 + k1 : 12 + k1]
                    part = part + jnp.where(mark, 0.0, t)
                    marks.append(jnp.where(mark, 1.0, 0.0))
                parts.append(part)
            turned[128 * pair : 128 * pair + 128, cols] = jnp.transpose(jnp.concatenate(parts, axis=0).astype(BF))
            if pair == 0:
                turned[512:640, cols] = jnp.transpose(jnp.concatenate(marks, axis=0).astype(BF))
    for n in range(4):
        cols = slice(512 * n, 512 * n + 512)
        p = jnp.concatenate([r[:, cols] for r in p_refs], axis=0)
        out_ref[:, cols] = jnp.dot(turned[...], p, preferred_element_type=F32).astype(out_ref.dtype)


def swap(v):
    return jnp.concatenate([v[:, 128 * (i ^ 1) : 128 * (i ^ 1) + 128] for i in range(8)], axis=1)


def aligned(v, t):
    picked = []
    for i in range(4):
        j, k = (i - t) % 4, (i + t) % 4
        picked += [v[:, 256 * j : 256 * j + 128], v[:, 256 * k + 128 : 256 * k + 256]]
    return jnp.concatenate(picked, axis=1)


def merge_kernel(t, raw, other, *refs):
    got = aligned(other[...], t) if t else swap(other[...])
    both = merge(unpack(raw[...]), unpack(got))
    refs[-1][...] = jnp.concatenate([*both, jnp.zeros((5, 1024), F32)], axis=0)


def block_kernel(k, mine, theirs, factor, *refs):
    got, out_ref = refs[0], refs[1 if k < 3 else 0]
    if k == 0:
        refs[2][...] = jnp.zeros((8, 128), F32)
    rows = slice(128 * k, 128 * k + 128)
    f = factor[...]
    for n in range(4):
        cols = slice(512 * n, 512 * n + 512)
        v = mine[rows, cols] * f[:, k : k + 1] + theirs[rows, cols].astype(F32) * f[:, 4 + k : 5 + k]
        if k == 0:
            v = v + (mine[512:640, cols] + theirs[512:640, cols].astype(F32)) * f[:, 8:9]
        if k < 3:
            v = v + got[:, cols].astype(F32)
        out_ref[:, cols] = v.astype(BF)


def gather_kernel(zero, one, two, three, *outs):
    for k in range(4):
        rows = slice(64 * k, 64 * k + 64)
        v = zero[rows] + two[rows].astype(F32) + (one[rows].astype(F32) + three[rows].astype(F32))
        outs[k][...] = v.astype(outs[k].dtype)


def last_kernel(a, b, c, d, _, out_ref):
    v = a[...] + c[...].astype(F32) + (b[...].astype(F32) + d[...].astype(F32))
    out_ref[...] = v.astype(BF)


def total_kernel(raw, other, stats, got, _, lse_ref, loss_ref, factor_ref):
    acc = merge(unpack(stats[...]), unpack(aligned(got[...], 2)))
    lse = acc[0] + jnp.log(acc[1])
    lse_ref[...] = jnp.broadcast_to(lse, (8, 1024))
    chosen = acc[2][:, 0:128]
    loss_ref[...] = lse[:, 0:128] - chosen
    rows = []
    for top in (raw[0:1, :], swap(other[...])[0:1]):
        f = jnp.exp(top - lse) * SHARP
        rows += [f[:, 256 * j : 256 * j + 128] for j in range(4)]
    pos = ((jnp.exp(chosen - lse[:, 0:128]) - 1.0) * SHARP).astype(BF).astype(F32)
    factor_ref[...] = jnp.transpose(jnp.concatenate([*rows, pos, jnp.zeros((119, 128), F32)], axis=0))


def coefficients(info, piece, t_ref, lse_ref, c_ref, at):
    step = steps(256)
    for pair in range(4):
        cols = slice(256 * pair, 256 * pair + 256)
        lse = lse_ref[0:1, cols]
        rows = info.rows(piece, pair, 0, 16)
        parts = []
        for k1 in range(4):
            part = jnp.where(step == rows[4 + k1 : 5 + k1], jnp.exp(rows[k1 : k1 + 1] - lse) * SHARP, 0.0)
            if pair == 0:
                t = t_ref[64 * k1 : 64 * k1 + 64, :] * jnp.exp(rows[8:9] - lse)
                t = t - jnp.where(step == rows[11 + k1 : 12 + k1], 1.0, 0.0)
                part = part + t * SHARP
            parts.append(part)
        c_ref[at : at + 256, cols] = jnp.concatenate(parts, axis=0).astype(BF)


def far_kernel(t_ref, *refs):
    infos, lse_ref, q_refs = refs[0:3], refs[3], refs[4:12]
    out_ref, c = refs[12:]
    coefficients(Info(*infos), 2, t_ref, lse_ref, c, 0)
    for n in range(4):
        cols = slice(512 * n, 512 * n + 512)
        q = jnp.concatenate([r[0:128, cols] for r in q_refs], axis=0)
        out_ref[:, cols] = jnp.dot(c[...], q, preferred_element_type=F32).astype(BF)


def near_kernel(*refs):
    ts, infos, lse_ref, q_refs = refs[0:3], refs[3:6], refs[6], refs[7:15]
    zero, one, three, c = refs[16:]
    info = Info(*infos)
    for i, piece in enumerate((0, 1, 3)):
        coefficients(info, piece, ts[i], lse_ref, c, 256 * i)
    for n in range(4):
        cols = slice(512 * n, 512 * n + 512)
        q = jnp.concatenate([r[0:128, cols] for r in q_refs], axis=0)
        g = jnp.dot(c[...], q, preferred_element_type=F32)
        zero[:, cols] = g[0:256]
        one[:, cols] = g[256:512].astype(BF)
        three[:, cols] = g[512:768].astype(BF)


def local(question_vectors, passages, positive, hard_owner, hard_row):
    packed = call(
        pack_kernel,
        shape(144, WIDTH, BF),
        [ANY] * 4,
        scratch=[
            pltpu.VMEM((16, 128), jnp.int32),
            pltpu.VMEM((16, 128), jnp.int32),
            pltpu.VMEM((1, 128), jnp.int32),
            pltpu.SemaphoreType.DMA((4,)),
        ],
        limit=56,
    )(question_vectors, hard_owner.T, hard_row.T, positive.reshape(1, 128))

    back = send(passages, first(1))
    ahead = send(passages, first(-1))
    across = send(passages, first(2))
    q1 = send(packed, along(1))
    mine0, kept = call(
        stage_kernel,
        (shape(144, WIDTH, BF), shape(64, WIDTH, BF)),
        [ANY, ANY],
        scratch=[pltpu.SemaphoreType.DMA((2,))],
    )(packed, passages)
    s0 = send(packed, CORE)
    back, ahead, across, q1, s0 = tied(back, ahead, across, q1, s0)
    plane = call(join_kernel, shape(256, WIDTH, BF), [VMEM] * 4)(kept, back, across, ahead)
    up = send(plane, second(1))
    down = send(plane, second(-1))
    over = send(plane, second(2))
    q2 = send(q1, along(1))
    q2, q1 = tied(q2, q1)
    s1 = send(q1, CORE)
    q3 = send(q2, along(1))
    s2 = send(q2, CORE)
    s3 = send(q3, CORE)
    tiles = (mine0, s0, q1, s1, q2, s2, q3, s3)

    pieces = (plane, up, over, down)
    tile = shape(256, 256, F32)

    def early(which):
        return call(
            lambda *r: early_kernel(which, *r),
            (tile, tile, shape(32, 768, F32)),
            [VMEM] * 8,
            2 * 512 * 768 * WIDTH,
        )(*[pieces[i] for i in which], *tiles[:6])

    t0, t3, soon = early(SOON)
    t1, t2, later = early(LATER)
    info_b, raw = call(
        late_kernel, (shape(64, 256, F32), shape(8, 1024, F32)), [VMEM] * 8, 2 * 1024 * 256 * WIDTH
    )(*pieces, *tiles[6:], soon, later)

    other = send(raw, CORE)
    stats = call(lambda *r: merge_kernel(0, *r), shape(8, 1024, F32), [VMEM] * 2)(raw, other)
    infos = (soon, later, info_b)
    operands = (t0, t1, t2, t3, *infos, raw, *pieces)

    def query(half, kind, after):
        return call(
            lambda *r: query_kernel(half, *r),
            shape(640, WIDTH, kind),
            [VMEM] * 13,
            2 * 640 * 1024 * WIDTH,
            scratch=[pltpu.VMEM((640, 1024), BF)],
        )(*operands, after)

    mine = query(0, F32, stats)
    both = call(lambda *r: merge_kernel(1, *r), shape(8, 1024, F32), [VMEM] * 3)(stats, send(stats, along(1)), mine)
    four = send(both, along(2))
    theirs = query(1, BF, both)
    lse, loss, factor = call(
        total_kernel, (shape(8, 1024, F32), shape(1, 128, F32), shape(128, 128, F32)), [VMEM] * 5
    )(raw, other, both, four, theirs)
    theirs, lse = tied(theirs, lse)
    theirs = send(theirs, CORE)

    far = call(far_kernel, shape(256, WIDTH, BF), [VMEM] * 13, 2 * 256 * 1024 * WIDTH, scratch=[pltpu.VMEM((256, 1024), BF)])(
        t2, *infos, lse, *tiles
    )
    two = send(far, second(2))

    zero, one, three = call(
        near_kernel,
        (shape(256, WIDTH, F32), shape(256, WIDTH, BF), shape(256, WIDTH, BF)),
        [VMEM] * 16,
        2 * 768 * 1024 * WIDTH,
        scratch=[pltpu.VMEM((768, 1024), BF)],
    )(t0, t1, t3, *infos, lse, *tiles, far)
    def block(k, *got):
        kernel = lambda *r: block_kernel(k, *r)
        outs = (shape(128, WIDTH, BF), shape(8, 128, F32)) if k == 0 else shape(128, WIDTH, BF)
        return call(kernel, outs, [VMEM] * (3 + len(got)))(mine, theirs, factor, *got)

    run = block(3)
    for k in (2, 1, 0):
        run = block(k, send(run, along(-1)))
    run, token = run

    one = send(one, second(-1))
    three = send(three, second(1))
    half = shape(64, WIDTH, BF)
    g0, g1, g2, g3 = call(gather_kernel, (shape(64, WIDTH, F32), half, half, half), [VMEM] * 4)(zero, one, two, three)
    g2 = send(g2, first(2))
    g1 = send(g1, first(-1))
    g3 = send(g3, first(1))
    passage_grad = call(last_kernel, half, [VMEM] * 5)(g0, g1, g2, g3, token)
    return loss.reshape(128), run, passage_grad


def solution(mesh):
    return jax.shard_map(
        local,
        mesh=mesh,
        in_specs=(P(AXES, None), P(AXES, None), P(AXES), P(AXES, None), P(AXES, None)),
        out_specs=(P(AXES), P(AXES, None), P(AXES, None)),
        check_vma=False,
    )
```

```python
import jax
import jax.numpy as jnp
from jax import lax
from jax.experimental import pallas as pl
from jax.experimental.pallas import tpu as pltpu
from jax.sharding import PartitionSpec as P

AXES = ("group", "dp")
SHARP = 1.0 / 0.02
FLOOR = -1e30
BF = jnp.bfloat16
F32 = jnp.float32
WIDTH = 2048
VMEM = pl.BlockSpec(memory_space=pltpu.VMEM)
ANY = pl.BlockSpec(memory_space=pl.ANY)


def index(y, x, z, c):
    return (((y % 4) * 4 + x % 4) * 4 + z % 4) * 2 + c % 2


def pairs(step):
    found = []
    for y in range(4):
        for x in range(4):
            for z in range(4):
                for c in range(2):
                    found.append((index(y, x, z, c), index(*step(y, x, z, c))))
    return found


def first(d):
    return pairs(lambda y, x, z, c: (y, x, z + d, c) if c else (y, x + d, z, c))


def second(d):
    return pairs(lambda y, x, z, c: (y, x + d, z, c) if c else (y, x, z + d, c))


def along(d):
    return pairs(lambda y, x, z, c: (y - d, x, z, c) if c else (y + d, x, z, c))


CORE = pairs(lambda y, x, z, c: (y, x, z, 1 - c))


def send(v, perm):
    return lax.ppermute(v, AXES, perm)


def tied(*v):
    return lax.optimization_barrier(v)


def join(*v):
    return jnp.concatenate(v, axis=0)


def call(kernel, outs, specs, flops=0, nbytes=0, scratch=(), limit=16):
    return pl.pallas_call(
        kernel,
        out_shape=outs,
        in_specs=specs,
        out_specs=jax.tree.map(lambda _: VMEM, outs),
        scratch_shapes=scratch,
        compiler_params=pltpu.CompilerParams(vmem_limit_bytes=limit * 2**20),
        cost_estimate=pl.CostEstimate(flops=flops, bytes_accessed=nbytes, transcendentals=0),
    )


def shape(r, c, t):
    return jax.ShapeDtypeStruct((r, c), t)


def pack_kernel(q_ref, owner_ref, row_ref, pos_ref, out_ref, owner, row, pos, sems):
    copies = []
    for i, (src, dst) in enumerate(
        ((owner_ref, owner), (row_ref, row), (pos_ref, pos), (q_ref, out_ref.at[0:128, :]))
    ):
        copies.append(pltpu.make_async_copy(src, dst, sems.at[i]))
        copies[-1].start()
    out_ref[128:144, 384:WIDTH] = jnp.zeros((16, WIDTH - 384), BF)
    for c in copies[:3]:
        c.wait()
    high = (pos[...] // 64).astype(F32)
    low = (pos[...] % 64).astype(F32)
    third = jnp.concatenate([high, low, jnp.zeros((14, 128), F32)], axis=0)
    meta = jnp.concatenate([owner[...].astype(F32), row[...].astype(F32), third], axis=1)
    out_ref[128:144, 0:384] = meta.astype(BF)
    copies[3].wait()


def stage_kernel(a_ref, b_ref, a_out, b_out, sems):
    one = pltpu.make_async_copy(a_ref, a_out, sems.at[0])
    two = pltpu.make_async_copy(b_ref, b_out, sems.at[1])
    one.start()
    two.start()
    one.wait()
    two.wait()


def join_kernel(*refs):
    for i, r in enumerate(refs[:4]):
        refs[4][64 * i : 64 * i + 64, :] = r[...]


def whereabouts():
    dp = lax.axis_index("dp")
    return lax.axis_index("group"), dp // 8, lax.rem(dp // 2, 4), lax.rem(dp, 2)


def owner_id(place, piece, k1):
    x, z, core = place[1], place[2], place[3]
    kx = jnp.where(core == 0, k1, piece)
    kz = jnp.where(core == 0, piece, k1)
    return (lax.rem(x - kx + 4, 4) * 4 + lax.rem(z - kz + 4, 4)) * 2 + core


PIECES = (0, 1, 2, 3)


def steps(n):
    return lax.broadcasted_iota(jnp.int32, (64, n), 0).astype(F32) + 1.0


def score_block(place, piece, pair, a, b, raw, t_ref, write):
    rows = []
    owners = jnp.concatenate([a[128:144, 0:128], b[128:144, 0:128]], axis=1).astype(F32)
    spots = jnp.concatenate([a[128:144, 128:256], b[128:144, 128:256]], axis=1).astype(F32) + 1.0
    step = steps(256)
    hard, where = [], []
    for k1 in range(4):
        whole = (place[0] * 32 + owner_id(place, piece, k1)).astype(F32)
        spot = jnp.sum(jnp.where(owners == whole, spots, 0.0), axis=0, keepdims=True)
        part = raw[64 * k1 : 64 * k1 + 64]
        found = jnp.sum(jnp.where(step == spot, part, 0.0), axis=0, keepdims=True) * SHARP
        hard.append(jnp.where(spot > 0, found, FLOOR))
        where.append(spot)
    top = jnp.maximum(jnp.maximum(hard[0], hard[1]), jnp.maximum(hard[2], hard[3]))
    chosen = jnp.zeros((1, 256), F32)
    marks = [chosen] * 4
    total = chosen
    if pair == 0:
        scores = raw * SHARP
        top = jnp.maximum(top, jnp.max(scores, axis=0, keepdims=True))
        t = jnp.exp(scores - top)
        t_ref[...] = t
        total = jnp.sum(t, axis=0, keepdims=True)
        pos = jnp.concatenate([a[128:144, 256:384], b[128:144, 256:384]], axis=1).astype(F32)
        marks = []
        for k1 in range(4):
            mine = owner_id(place, piece, k1).astype(F32)
            mark = jnp.where(pos[0:1] == mine, pos[1:2] + 1.0, 0.0)
            part = scores[64 * k1 : 64 * k1 + 64]
            chosen = chosen + jnp.sum(jnp.where(step == mark, part, 0.0), axis=0, keepdims=True)
            marks.append(mark)
    for k1 in range(4):
        total = total + jnp.where(where[k1] > 0, jnp.exp(hard[k1] - top), 0.0)
    write(jnp.concatenate([*hard, *where, top, total, chosen, *marks, jnp.zeros((1, 256), F32)], axis=0))


def product(p, a, b):
    q = jnp.concatenate([a[0:128, :], b[0:128, :]], axis=0)
    return lax.dot_general(p, q, (((1,), (1,)), ((), ())), preferred_element_type=F32)


def writer(ref, rows, cols):
    def write(v):
        ref[rows : rows + 16, cols : cols + 256] = v

    return write


def early_kernel(pieces, *refs):
    p_refs, q_refs, ts, info = refs[0:2], refs[2:8], refs[8:10], refs[10]
    place = whereabouts()
    p = jnp.concatenate([r[...] for r in p_refs], axis=0)
    for pair in range(3):
        a, b = q_refs[2 * pair], q_refs[2 * pair + 1]
        raw = product(p, a, b)
        for i, piece in enumerate(pieces):
            part = raw[256 * i : 256 * i + 256]
            score_block(place, piece, pair, a, b, part, ts[i], writer(info, 16 * i, 256 * pair))


SOON, LATER = (0, 2), (1, 3)


class Info:
    def __init__(self, *refs):
        self.refs = refs

    def rows(self, piece, pair, first, last):
        if pair < 3:
            ref = self.refs[0 if piece in SOON else 1]
            i = 16 * (SOON if piece in SOON else LATER).index(piece)
            return ref[i + first : i + last, 256 * pair : 256 * pair + 256]
        i = 16 * piece
        return self.refs[2][i + first : i + last, 0:256]


def merge(a, b):
    top = jnp.maximum(a[0], b[0])
    total = a[1] * jnp.exp(a[0] - top) + b[1] * jnp.exp(b[0] - top)
    return top, total, a[2] + b[2]


def unpack(v):
    return v[0:1], v[1:2], v[2:3]


def late_kernel(*refs):
    p_refs, q_refs, soon, later, info_b, stats_ref = refs[0:4], refs[4:6], *refs[6:10]
    place = whereabouts()
    p = jnp.concatenate([r[...] for r in p_refs], axis=0)
    raw = product(p, q_refs[0], q_refs[1])
    for i in PIECES:
        part = raw[256 * i : 256 * i + 256]
        score_block(place, i, 3, q_refs[0], q_refs[1], part, None, writer(info_b, 16 * i, 0))
    info = Info(soon, later, info_b)
    for pair in range(4):
        acc = unpack(info.rows(0, pair, 8, 11))
        for piece in (1, 2, 3):
            acc = merge(acc, unpack(info.rows(piece, pair, 8, 11)))
        stats_ref[:, 256 * pair : 256 * pair + 256] = jnp.concatenate([*acc, jnp.zeros((5, 256), F32)], axis=0)


def query_kernel(half, *refs):
    ts, infos, stats, p_refs, out_ref, turned = refs[0:4], refs[4:7], refs[7], refs[8:12], refs[13], refs[14]
    info = Info(*infos)
    step = steps(128)
    side = slice(128 * half, 128 * half + 128)
    for piece in PIECES:
        cols = slice(256 * piece, 256 * piece + 256)
        for pair in range(4):
            top = stats[0:1, 256 * pair + 128 * half : 256 * pair + 128 * half + 128]
            rows = info.rows(piece, pair, 0, 16)[:, side]
            parts = []
            marks = []
            for k1 in range(4):
                part = jnp.where(step == rows[4 + k1 : 5 + k1], jnp.exp(rows[k1 : k1 + 1] - top), 0.0)
                if pair == 0:
                    t = ts[piece][64 * k1 : 64 * k1 + 64, side] * jnp.exp(rows[8:9] - top)
                    mark = step == rows[11 + k1 : 12 + k1]
                    part = part + jnp.where(mark, 0.0, t)
                    marks.append(jnp.where(mark, 1.0, 0.0))
                parts.append(part)
            turned[128 * pair : 128 * pair + 128, cols] = jnp.transpose(jnp.concatenate(parts, axis=0).astype(BF))
            if pair == 0:
                turned[512:640, cols] = jnp.transpose(jnp.concatenate(marks, axis=0).astype(BF))
    for n in range(4):
        cols = slice(512 * n, 512 * n + 512)
        p = jnp.concatenate([r[:, cols] for r in p_refs], axis=0)
        out_ref[:, cols] = jnp.dot(turned[...], p, preferred_element_type=F32).astype(out_ref.dtype)


def swap(v):
    return jnp.concatenate([v[:, 128 * (i ^ 1) : 128 * (i ^ 1) + 128] for i in range(8)], axis=1)


def aligned(v, t):
    picked = []
    for i in range(4):
        j, k = (i - t) % 4, (i + t) % 4
        picked += [v[:, 256 * j : 256 * j + 128], v[:, 256 * k + 128 : 256 * k + 256]]
    return jnp.concatenate(picked, axis=1)


def merge_kernel(t, raw, other, *refs):
    got = aligned(other[...], t) if t else swap(other[...])
    both = merge(unpack(raw[...]), unpack(got))
    refs[-1][...] = jnp.concatenate([*both, jnp.zeros((5, 1024), F32)], axis=0)


def block_kernel(k, mine, theirs, factor, extra, *refs):
    got, out_ref = refs[0], refs[1 if k < 3 else 0]
    if k == 0:
        refs[2][...] = jnp.zeros((8, 128), F32)
        refs[3][...] = extra[1:2, 0:128]
    rows = slice(128 * k, 128 * k + 128)
    f = factor[...]
    for n in range(4):
        cols = slice(512 * n, 512 * n + 512)
        v = mine[rows, cols] * f[:, k : k + 1] + theirs[rows, cols].astype(F32) * f[:, 4 + k : 5 + k]
        if k == 0:
            v = v + (mine[512:640, cols] + theirs[512:640, cols].astype(F32)) * f[:, 8:9]
        if k < 3:
            v = v + got[:, cols].astype(F32)
        out_ref[:, cols] = v.astype(BF)


def gather_kernel(zero, one, two, three, *outs):
    for k in range(4):
        rows = slice(64 * k, 64 * k + 64)
        v = zero[rows] + two[rows].astype(F32) + (one[rows].astype(F32) + three[rows].astype(F32))
        outs[k][...] = v.astype(outs[k].dtype)


def last_kernel(a, b, c, d, _, out_ref):
    v = a[...] + c[...].astype(F32) + (b[...].astype(F32) + d[...].astype(F32))
    out_ref[...] = v.astype(BF)


def total_kernel(raw, other, stats, got, _, lse_ref, factor_ref):
    acc = merge(unpack(stats[...]), unpack(aligned(got[...], 2)))
    lse = acc[0] + jnp.log(acc[1])
    chosen = acc[2][:, 0:128]
    loss = jnp.concatenate([lse[:, 0:128] - chosen, jnp.zeros((1, 896), F32)], axis=1)
    lse_ref[...] = jnp.concatenate([lse, loss, jnp.zeros((6, 1024), F32)], axis=0)
    rows = []
    for top in (raw[0:1, :], swap(other[...])[0:1]):
        f = jnp.exp(top - lse) * SHARP
        rows += [f[:, 256 * j : 256 * j + 128] for j in range(4)]
    pos = ((jnp.exp(chosen - lse[:, 0:128]) - 1.0) * SHARP).astype(BF).astype(F32)
    factor_ref[...] = jnp.transpose(jnp.concatenate([*rows, pos, jnp.zeros((119, 128), F32)], axis=0))


def coefficients(info, piece, t_ref, lse_ref, c_ref, at):
    step = steps(256)
    for pair in range(4):
        cols = slice(256 * pair, 256 * pair + 256)
        lse = lse_ref[0:1, cols]
        rows = info.rows(piece, pair, 0, 16)
        parts = []
        for k1 in range(4):
            part = jnp.where(step == rows[4 + k1 : 5 + k1], jnp.exp(rows[k1 : k1 + 1] - lse) * SHARP, 0.0)
            if pair == 0:
                t = t_ref[64 * k1 : 64 * k1 + 64, :] * jnp.exp(rows[8:9] - lse)
                t = t - jnp.where(step == rows[11 + k1 : 12 + k1], 1.0, 0.0)
                part = part + t * SHARP
            parts.append(part)
        c_ref[at : at + 256, cols] = jnp.concatenate(parts, axis=0).astype(BF)


def far_kernel(t_ref, *refs):
    infos, lse_ref, q_refs = refs[0:3], refs[3], refs[4:12]
    out_ref, c = refs[12:]
    coefficients(Info(*infos), 2, t_ref, lse_ref, c, 0)
    for n in range(4):
        cols = slice(512 * n, 512 * n + 512)
        q = jnp.concatenate([r[0:128, cols] for r in q_refs], axis=0)
        out_ref[:, cols] = jnp.dot(c[...], q, preferred_element_type=F32).astype(BF)


def near_kernel(*refs):
    ts, infos, lse_ref, q_refs = refs[0:3], refs[3:6], refs[6], refs[7:15]
    zero, one, three, c = refs[16:]
    info = Info(*infos)
    for i, piece in enumerate((0, 1, 3)):
        coefficients(info, piece, ts[i], lse_ref, c, 256 * i)
    for n in range(4):
        cols = slice(512 * n, 512 * n + 512)
        q = jnp.concatenate([r[0:128, cols] for r in q_refs], axis=0)
        g = jnp.dot(c[...], q, preferred_element_type=F32)
        zero[:, cols] = g[0:256]
        one[:, cols] = g[256:512].astype(BF)
        three[:, cols] = g[512:768].astype(BF)


def local(question_vectors, passages, positive, hard_owner, hard_row):
    packed = call(
        pack_kernel,
        shape(144, WIDTH, BF),
        [ANY] * 4,
        scratch=[
            pltpu.VMEM((16, 128), jnp.int32),
            pltpu.VMEM((16, 128), jnp.int32),
            pltpu.VMEM((1, 128), jnp.int32),
            pltpu.SemaphoreType.DMA((4,)),
        ],
        limit=56,
    )(question_vectors, hard_owner.T, hard_row.T, positive.reshape(1, 128))

    back = send(passages, first(1))
    ahead = send(passages, first(-1))
    across = send(passages, first(2))
    q1 = send(packed, along(1))
    mine0, kept = call(
        stage_kernel,
        (shape(144, WIDTH, BF), shape(64, WIDTH, BF)),
        [ANY, ANY],
        scratch=[pltpu.SemaphoreType.DMA((2,))],
    )(packed, passages)
    s0 = send(packed, CORE)
    back, ahead, across, q1, s0 = tied(back, ahead, across, q1, s0)
    plane = call(join_kernel, shape(256, WIDTH, BF), [VMEM] * 4)(kept, back, across, ahead)
    up = send(plane, second(1))
    down = send(plane, second(-1))
    over = send(plane, second(2))
    q2 = send(q1, along(1))
    q2, q1 = tied(q2, q1)
    s1 = send(q1, CORE)
    q3 = send(q2, along(1))
    s2 = send(q2, CORE)
    s3 = send(q3, CORE)
    tiles = (mine0, s0, q1, s1, q2, s2, q3, s3)

    pieces = (plane, up, over, down)
    tile = shape(256, 256, F32)

    def early(which):
        return call(
            lambda *r: early_kernel(which, *r),
            (tile, tile, shape(32, 768, F32)),
            [VMEM] * 8,
            2 * 512 * 768 * WIDTH,
        )(*[pieces[i] for i in which], *tiles[:6])

    t0, t2, soon = early(SOON)
    t1, t3, later = early(LATER)
    info_b, raw = call(
        late_kernel, (shape(64, 256, F32), shape(8, 1024, F32)), [VMEM] * 8, 2 * 1024 * 256 * WIDTH
    )(*pieces, *tiles[6:], soon, later)

    other = send(raw, CORE)
    stats = call(lambda *r: merge_kernel(0, *r), shape(8, 1024, F32), [VMEM] * 2)(raw, other)
    infos = (soon, later, info_b)
    operands = (t0, t1, t2, t3, *infos, raw, *pieces)

    def query(half, kind, after):
        return call(
            lambda *r: query_kernel(half, *r),
            shape(640, WIDTH, kind),
            [VMEM] * 13,
            2 * 640 * 1024 * WIDTH,
            scratch=[pltpu.VMEM((640, 1024), BF)],
        )(*operands, after)

    mine = query(0, F32, stats)
    both = call(lambda *r: merge_kernel(1, *r), shape(8, 1024, F32), [VMEM] * 3)(stats, send(stats, along(1)), mine)
    four = send(both, along(2))
    theirs = query(1, BF, both)
    lse, factor = call(
        total_kernel, (shape(8, 1024, F32), shape(128, 128, F32)), [VMEM] * 5
    )(raw, other, both, four, theirs)
    theirs, lse = tied(theirs, lse)
    theirs = send(theirs, CORE)

    far = call(far_kernel, shape(256, WIDTH, BF), [VMEM] * 13, 2 * 256 * 1024 * WIDTH, scratch=[pltpu.VMEM((256, 1024), BF)])(
        t2, *infos, lse, *tiles
    )
    two = send(far, second(2))

    zero, one, three = call(
        near_kernel,
        (shape(256, WIDTH, F32), shape(256, WIDTH, BF), shape(256, WIDTH, BF)),
        [VMEM] * 16,
        2 * 768 * 1024 * WIDTH,
        scratch=[pltpu.VMEM((768, 1024), BF)],
    )(t0, t1, t3, *infos, lse, *tiles, theirs)
    def block(k, *got):
        kernel = lambda *r: block_kernel(k, *r)
        outs = (shape(128, WIDTH, BF), shape(8, 128, F32), shape(1, 128, F32)) if k == 0 else shape(128, WIDTH, BF)
        return call(kernel, outs, [VMEM] * (4 + len(got)))(mine, theirs, factor, lse, *got)

    run = block(3)
    for k in (2, 1, 0):
        run = block(k, send(run, along(-1)))
    run, token, loss = run

    one = send(one, second(-1))
    three = send(three, second(1))
    half = shape(64, WIDTH, BF)
    g0, g1, g2, g3 = call(gather_kernel, (shape(64, WIDTH, F32), half, half, half), [VMEM] * 4)(zero, one, two, three)
    g2 = send(g2, first(2))
    g1 = send(g1, first(-1))
    g3 = send(g3, first(1))
    passage_grad = call(last_kernel, half, [VMEM] * 5)(g0, g1, g2, g3, token)
    return loss.reshape(128), run, passage_grad


def solution(mesh):
    return jax.shard_map(
        local,
        mesh=mesh,
        in_specs=(P(AXES, None), P(AXES, None), P(AXES), P(AXES, None), P(AXES, None)),
        out_specs=(P(AXES), P(AXES, None), P(AXES, None)),
        check_vma=False,
    )
```

```python
import jax
import jax.numpy as jnp
from jax import lax
from jax.experimental import pallas as pl
from jax.experimental.pallas import tpu as pltpu
from jax.sharding import PartitionSpec as P

AXES = ("group", "dp")
SHARP = 1.0 / 0.02
FLOOR = -1e30
BF = jnp.bfloat16
F32 = jnp.float32
WIDTH = 2048
VMEM = pl.BlockSpec(memory_space=pltpu.VMEM)
ANY = pl.BlockSpec(memory_space=pl.ANY)


def index(y, x, z, c):
    return (((y % 4) * 4 + x % 4) * 4 + z % 4) * 2 + c % 2


def pairs(step):
    found = []
    for y in range(4):
        for x in range(4):
            for z in range(4):
                for c in range(2):
                    found.append((index(y, x, z, c), index(*step(y, x, z, c))))
    return found


def first(d):
    return pairs(lambda y, x, z, c: (y, x, z + d, c) if c else (y, x + d, z, c))


def second(d):
    return pairs(lambda y, x, z, c: (y, x + d, z, c) if c else (y, x, z + d, c))


def along(d):
    return pairs(lambda y, x, z, c: (y - d, x, z, c) if c else (y + d, x, z, c))


CORE = pairs(lambda y, x, z, c: (y, x, z, 1 - c))


def send(v, perm):
    return lax.ppermute(v, AXES, perm)


def tied(*v):
    return lax.optimization_barrier(v)


def join(*v):
    return jnp.concatenate(v, axis=0)


def call(kernel, outs, specs, flops=0, nbytes=0, scratch=(), limit=16):
    return pl.pallas_call(
        kernel,
        out_shape=outs,
        in_specs=specs,
        out_specs=jax.tree.map(lambda _: VMEM, outs),
        scratch_shapes=scratch,
        compiler_params=pltpu.CompilerParams(vmem_limit_bytes=limit * 2**20),
        cost_estimate=pl.CostEstimate(flops=flops, bytes_accessed=nbytes, transcendentals=0),
    )


def shape(r, c, t):
    return jax.ShapeDtypeStruct((r, c), t)


def pack_kernel(q_ref, owner_ref, row_ref, pos_ref, out_ref, owner, row, pos, sems):
    copies = []
    for i, (src, dst) in enumerate(
        ((owner_ref, owner), (row_ref, row), (pos_ref, pos), (q_ref, out_ref.at[0:128, :]))
    ):
        copies.append(pltpu.make_async_copy(src, dst, sems.at[i]))
        copies[-1].start()
    out_ref[128:144, 384:WIDTH] = jnp.zeros((16, WIDTH - 384), BF)
    for c in copies[:3]:
        c.wait()
    high = (pos[...] // 64).astype(F32)
    low = (pos[...] % 64).astype(F32)
    third = jnp.concatenate([high, low, jnp.zeros((14, 128), F32)], axis=0)
    meta = jnp.concatenate([owner[...].astype(F32), row[...].astype(F32), third], axis=1)
    out_ref[128:144, 0:384] = meta.astype(BF)
    copies[3].wait()


def stage_kernel(a_ref, b_ref, a_out, b_out, sems):
    one = pltpu.make_async_copy(a_ref, a_out, sems.at[0])
    two = pltpu.make_async_copy(b_ref, b_out, sems.at[1])
    one.start()
    two.start()
    one.wait()
    two.wait()


def join_kernel(*refs):
    for i, r in enumerate(refs[:4]):
        refs[4][64 * i : 64 * i + 64, :] = r[...]


def whereabouts():
    dp = lax.axis_index("dp")
    return lax.axis_index("group"), dp // 8, lax.rem(dp // 2, 4), lax.rem(dp, 2)


def owner_id(place, piece, k1):
    x, z, core = place[1], place[2], place[3]
    kx = jnp.where(core == 0, k1, piece)
    kz = jnp.where(core == 0, piece, k1)
    return (lax.rem(x - kx + 4, 4) * 4 + lax.rem(z - kz + 4, 4)) * 2 + core


PIECES = (0, 1, 2, 3)


def steps(n):
    return lax.broadcasted_iota(jnp.int32, (64, n), 0).astype(F32) + 1.0


def score_block(place, piece, pair, a, b, raw, t_ref, write):
    rows = []
    owners = jnp.concatenate([a[128:144, 0:128], b[128:144, 0:128]], axis=1).astype(F32)
    spots = jnp.concatenate([a[128:144, 128:256], b[128:144, 128:256]], axis=1).astype(F32) + 1.0
    step = steps(256)
    hard, where = [], []
    for k1 in range(4):
        whole = (place[0] * 32 + owner_id(place, piece, k1)).astype(F32)
        spot = jnp.sum(jnp.where(owners == whole, spots, 0.0), axis=0, keepdims=True)
        part = raw[64 * k1 : 64 * k1 + 64]
        found = jnp.sum(jnp.where(step == spot, part, 0.0), axis=0, keepdims=True) * SHARP
        hard.append(jnp.where(spot > 0, found, FLOOR))
        where.append(spot)
    top = jnp.maximum(jnp.maximum(hard[0], hard[1]), jnp.maximum(hard[2], hard[3]))
    chosen = jnp.zeros((1, 256), F32)
    marks = [chosen] * 4
    total = chosen
    if pair == 0:
        scores = raw * SHARP
        top = jnp.maximum(top, jnp.max(scores, axis=0, keepdims=True))
        t = jnp.exp(scores - top)
        t_ref[...] = t
        total = jnp.sum(t, axis=0, keepdims=True)
        pos = jnp.concatenate([a[128:144, 256:384], b[128:144, 256:384]], axis=1).astype(F32)
        marks = []
        for k1 in range(4):
            mine = owner_id(place, piece, k1).astype(F32)
            mark = jnp.where(pos[0:1] == mine, pos[1:2] + 1.0, 0.0)
            part = scores[64 * k1 : 64 * k1 + 64]
            chosen = chosen + jnp.sum(jnp.where(step == mark, part, 0.0), axis=0, keepdims=True)
            marks.append(mark)
    for k1 in range(4):
        total = total + jnp.where(where[k1] > 0, jnp.exp(hard[k1] - top), 0.0)
    write(jnp.concatenate([*hard, *where, top, total, chosen, *marks, jnp.zeros((1, 256), F32)], axis=0))


def product(p, a, b):
    q = jnp.concatenate([a[0:128, :], b[0:128, :]], axis=0)
    return lax.dot_general(p, q, (((1,), (1,)), ((), ())), preferred_element_type=F32)


def writer(ref, rows, cols):
    def write(v):
        ref[rows : rows + 16, cols : cols + 256] = v

    return write


def early_kernel(pieces, *refs):
    p_refs, q_refs, ts, info = refs[0:2], refs[2:8], refs[8:10], refs[10]
    place = whereabouts()
    p = jnp.concatenate([r[...] for r in p_refs], axis=0)
    for pair in range(3):
        a, b = q_refs[2 * pair], q_refs[2 * pair + 1]
        raw = product(p, a, b)
        for i, piece in enumerate(pieces):
            part = raw[256 * i : 256 * i + 256]
            score_block(place, piece, pair, a, b, part, ts[i], writer(info, 16 * i, 256 * pair))


SOON, LATER = (0, 2), (1, 3)


class Info:
    def __init__(self, *refs):
        self.refs = refs

    def rows(self, piece, pair, first, last):
        if pair < 3:
            ref = self.refs[0 if piece in SOON else 1]
            i = 16 * (SOON if piece in SOON else LATER).index(piece)
            return ref[i + first : i + last, 256 * pair : 256 * pair + 256]
        i = 16 * piece
        return self.refs[2][i + first : i + last, 0:256]


def merge(a, b):
    top = jnp.maximum(a[0], b[0])
    total = a[1] * jnp.exp(a[0] - top) + b[1] * jnp.exp(b[0] - top)
    return top, total, a[2] + b[2]


def unpack(v):
    return v[0:1], v[1:2], v[2:3]


def late_kernel(*refs):
    p_refs, q_refs, soon, later, info_b, stats_ref = refs[0:4], refs[4:6], *refs[6:10]
    place = whereabouts()
    p = jnp.concatenate([r[...] for r in p_refs], axis=0)
    raw = product(p, q_refs[0], q_refs[1])
    for i in PIECES:
        part = raw[256 * i : 256 * i + 256]
        score_block(place, i, 3, q_refs[0], q_refs[1], part, None, writer(info_b, 16 * i, 0))
    info = Info(soon, later, info_b)
    for pair in range(4):
        acc = unpack(info.rows(0, pair, 8, 11))
        for piece in (1, 2, 3):
            acc = merge(acc, unpack(info.rows(piece, pair, 8, 11)))
        stats_ref[:, 256 * pair : 256 * pair + 256] = jnp.concatenate([*acc, jnp.zeros((5, 256), F32)], axis=0)


def query_kernel(half, *refs):
    ts, infos, stats, p_refs, out_ref, turned = refs[0:4], refs[4:7], refs[7], refs[8:12], refs[13], refs[14]
    info = Info(*infos)
    step = steps(128)
    side = slice(128 * half, 128 * half + 128)
    for piece in PIECES:
        cols = slice(256 * piece, 256 * piece + 256)
        for pair in range(4):
            top = stats[0:1, 256 * pair + 128 * half : 256 * pair + 128 * half + 128]
            rows = info.rows(piece, pair, 0, 16)[:, side]
            parts = []
            marks = []
            for k1 in range(4):
                part = jnp.where(step == rows[4 + k1 : 5 + k1], jnp.exp(rows[k1 : k1 + 1] - top), 0.0)
                if pair == 0:
                    t = ts[piece][64 * k1 : 64 * k1 + 64, side] * jnp.exp(rows[8:9] - top)
                    mark = step == rows[11 + k1 : 12 + k1]
                    part = part + jnp.where(mark, 0.0, t)
                    marks.append(jnp.where(mark, 1.0, 0.0))
                parts.append(part)
            turned[128 * pair : 128 * pair + 128, cols] = jnp.transpose(jnp.concatenate(parts, axis=0).astype(BF))
            if pair == 0:
                turned[512:640, cols] = jnp.transpose(jnp.concatenate(marks, axis=0).astype(BF))
    for n in range(4):
        cols = slice(512 * n, 512 * n + 512)
        p = jnp.concatenate([r[:, cols] for r in p_refs], axis=0)
        out_ref[:, cols] = jnp.dot(turned[...], p, preferred_element_type=F32).astype(out_ref.dtype)


def swap(v):
    return jnp.concatenate([v[:, 128 * (i ^ 1) : 128 * (i ^ 1) + 128] for i in range(8)], axis=1)


def aligned(v, t):
    picked = []
    for i in range(4):
        j, k = (i - t) % 4, (i + t) % 4
        picked += [v[:, 256 * j : 256 * j + 128], v[:, 256 * k + 128 : 256 * k + 256]]
    return jnp.concatenate(picked, axis=1)


def merge_kernel(t, raw, other, *refs):
    got = aligned(other[...], t) if t else swap(other[...])
    both = merge(unpack(raw[...]), unpack(got))
    refs[-1][...] = jnp.concatenate([*both, jnp.zeros((5, 1024), F32)], axis=0)


def block_kernel(k, mine, theirs, factor, extra, *refs):
    got, out_ref = refs[0], refs[1 if k < 3 else 0]
    if k == 0:
        refs[2][...] = jnp.zeros((8, 128), F32)
        refs[3][...] = extra[1:2, 0:128]
    rows = slice(128 * k, 128 * k + 128)
    f = factor[...]
    for n in range(4):
        cols = slice(512 * n, 512 * n + 512)
        v = mine[rows, cols] * f[:, k : k + 1] + theirs[rows, cols].astype(F32) * f[:, 4 + k : 5 + k]
        if k == 0:
            v = v + (mine[512:640, cols] + theirs[512:640, cols].astype(F32)) * f[:, 8:9]
        if k < 3:
            v = v + got[:, cols].astype(F32)
        out_ref[:, cols] = v.astype(BF)


def gather_kernel(zero, one, two, three, *outs):
    for k in range(4):
        rows = slice(64 * k, 64 * k + 64)
        v = zero[rows] + two[rows].astype(F32) + (one[rows].astype(F32) + three[rows].astype(F32))
        outs[k][...] = v.astype(outs[k].dtype)


def last_kernel(a, b, c, d, _, out_ref):
    v = a[...] + b[...].astype(F32) + (c[...].astype(F32) + d[...].astype(F32))
    out_ref[...] = v.astype(BF)


def total_kernel(raw, other, stats, got, _, lse_ref, factor_ref):
    acc = merge(unpack(stats[...]), unpack(aligned(got[...], 2)))
    lse = acc[0] + jnp.log(acc[1])
    chosen = acc[2][:, 0:128]
    loss = jnp.concatenate([lse[:, 0:128] - chosen, jnp.zeros((1, 896), F32)], axis=1)
    lse_ref[...] = jnp.concatenate([lse, loss, jnp.zeros((6, 1024), F32)], axis=0)
    rows = []
    for top in (raw[0:1, :], swap(other[...])[0:1]):
        f = jnp.exp(top - lse) * SHARP
        rows += [f[:, 256 * j : 256 * j + 128] for j in range(4)]
    pos = ((jnp.exp(chosen - lse[:, 0:128]) - 1.0) * SHARP).astype(BF).astype(F32)
    factor_ref[...] = jnp.transpose(jnp.concatenate([*rows, pos, jnp.zeros((119, 128), F32)], axis=0))


def coefficients(info, piece, t_ref, lse_ref, c_ref, at):
    step = steps(256)
    for pair in range(4):
        cols = slice(256 * pair, 256 * pair + 256)
        lse = lse_ref[0:1, cols]
        rows = info.rows(piece, pair, 0, 16)
        parts = []
        for k1 in range(4):
            part = jnp.where(step == rows[4 + k1 : 5 + k1], jnp.exp(rows[k1 : k1 + 1] - lse) * SHARP, 0.0)
            if pair == 0:
                t = t_ref[64 * k1 : 64 * k1 + 64, :] * jnp.exp(rows[8:9] - lse)
                t = t - jnp.where(step == rows[11 + k1 : 12 + k1], 1.0, 0.0)
                part = part + t * SHARP
            parts.append(part)
        c_ref[at : at + 256, cols] = jnp.concatenate(parts, axis=0).astype(BF)


def far_kernel(t_ref, *refs):
    infos, lse_ref, q_refs = refs[0:3], refs[3], refs[4:12]
    out_ref, c = refs[12:]
    coefficients(Info(*infos), 2, t_ref, lse_ref, c, 0)
    for n in range(4):
        cols = slice(512 * n, 512 * n + 512)
        q = jnp.concatenate([r[0:128, cols] for r in q_refs], axis=0)
        out_ref[:, cols] = jnp.dot(c[...], q, preferred_element_type=F32).astype(BF)


def near_kernel(*refs):
    ts, infos, lse_ref, q_refs = refs[0:3], refs[3:6], refs[6], refs[7:15]
    zero, one, three, c = refs[16:]
    info = Info(*infos)
    for i, piece in enumerate((0, 1, 3)):
        coefficients(info, piece, ts[i], lse_ref, c, 256 * i)
    for n in range(4):
        cols = slice(512 * n, 512 * n + 512)
        q = jnp.concatenate([r[0:128, cols] for r in q_refs], axis=0)
        g = jnp.dot(c[...], q, preferred_element_type=F32)
        zero[:, cols] = g[0:256]
        one[:, cols] = g[256:512].astype(BF)
        three[:, cols] = g[512:768].astype(BF)


def local(question_vectors, passages, positive, hard_owner, hard_row):
    packed = call(
        pack_kernel,
        shape(144, WIDTH, BF),
        [ANY] * 4,
        scratch=[
            pltpu.VMEM((16, 128), jnp.int32),
            pltpu.VMEM((16, 128), jnp.int32),
            pltpu.VMEM((1, 128), jnp.int32),
            pltpu.SemaphoreType.DMA((4,)),
        ],
        limit=56,
    )(question_vectors, hard_owner.T, hard_row.T, positive.reshape(1, 128))

    back = send(passages, first(1))
    ahead = send(passages, first(-1))
    across = send(passages, first(2))
    q1 = send(packed, along(1))
    mine0, kept = call(
        stage_kernel,
        (shape(144, WIDTH, BF), shape(64, WIDTH, BF)),
        [ANY, ANY],
        scratch=[pltpu.SemaphoreType.DMA((2,))],
    )(packed, passages)
    s0 = send(packed, CORE)
    across, back, ahead, q1, s0 = tied(across, back, ahead, q1, s0)
    plane = call(join_kernel, shape(256, WIDTH, BF), [VMEM] * 4)(kept, back, across, ahead)
    up = send(plane, second(1))
    down = send(plane, second(-1))
    over = send(plane, second(2))
    q2 = send(q1, along(1))
    q2, q1 = tied(q2, q1)
    s1 = send(q1, CORE)
    q3 = send(q2, along(1))
    s2 = send(q2, CORE)
    s3 = send(q3, CORE)
    tiles = (mine0, s0, q1, s1, q2, s2, q3, s3)

    pieces = (plane, up, over, down)
    tile = shape(256, 256, F32)

    def early(which):
        return call(
            lambda *r: early_kernel(which, *r),
            (tile, tile, shape(32, 768, F32)),
            [VMEM] * 8,
            2 * 512 * 768 * WIDTH,
        )(*[pieces[i] for i in which], *tiles[:6])

    t0, t2, soon = early(SOON)
    t1, t3, later = early(LATER)
    info_b, raw = call(
        late_kernel, (shape(64, 256, F32), shape(8, 1024, F32)), [VMEM] * 8, 2 * 1024 * 256 * WIDTH
    )(*pieces, *tiles[6:], soon, later)

    other = send(raw, CORE)
    stats = call(lambda *r: merge_kernel(0, *r), shape(8, 1024, F32), [VMEM] * 2)(raw, other)
    infos = (soon, later, info_b)
    operands = (t0, t1, t2, t3, *infos, raw, *pieces)

    def query(half, kind, after):
        return call(
            lambda *r: query_kernel(half, *r),
            shape(640, WIDTH, kind),
            [VMEM] * 13,
            2 * 640 * 1024 * WIDTH,
            scratch=[pltpu.VMEM((640, 1024), BF)],
        )(*operands, after)

    mine = query(0, F32, stats)
    both = call(lambda *r: merge_kernel(1, *r), shape(8, 1024, F32), [VMEM] * 3)(stats, send(stats, along(1)), mine)
    four = send(both, along(2))
    theirs = query(1, BF, both)
    lse, factor = call(
        total_kernel, (shape(8, 1024, F32), shape(128, 128, F32)), [VMEM] * 5
    )(raw, other, both, four, theirs)
    theirs, lse = tied(theirs, lse)
    theirs = send(theirs, CORE)

    far = call(far_kernel, shape(256, WIDTH, BF), [VMEM] * 13, 2 * 256 * 1024 * WIDTH, scratch=[pltpu.VMEM((256, 1024), BF)])(
        t2, *infos, lse, *tiles
    )
    two = send(far, second(2))

    zero, one, three = call(
        near_kernel,
        (shape(256, WIDTH, F32), shape(256, WIDTH, BF), shape(256, WIDTH, BF)),
        [VMEM] * 16,
        2 * 768 * 1024 * WIDTH,
        scratch=[pltpu.VMEM((768, 1024), BF)],
    )(t0, t1, t3, *infos, lse, *tiles, theirs)
    def block(k, *got):
        kernel = lambda *r: block_kernel(k, *r)
        outs = (shape(128, WIDTH, BF), shape(8, 128, F32), shape(1, 128, F32)) if k == 0 else shape(128, WIDTH, BF)
        return call(kernel, outs, [VMEM] * (4 + len(got)))(mine, theirs, factor, lse, *got)

    run = block(3)
    for k in (2, 1, 0):
        run = block(k, send(run, along(-1)))
    run, token, loss = run

    one = send(one, second(-1))
    three = send(three, second(1))
    half = shape(64, WIDTH, BF)
    g0, g1, g2, g3 = call(gather_kernel, (shape(64, WIDTH, F32), half, half, half), [VMEM] * 4)(zero, one, two, three)
    g2 = send(g2, first(2))
    g1 = send(g1, first(-1))
    g3 = send(g3, first(1))
    passage_grad = call(last_kernel, half, [VMEM] * 5)(g0, g2, g1, g3, token)
    return loss.reshape(128), run, passage_grad


def solution(mesh):
    return jax.shard_map(
        local,
        mesh=mesh,
        in_specs=(P(AXES, None), P(AXES, None), P(AXES), P(AXES, None), P(AXES, None)),
        out_specs=(P(AXES), P(AXES, None), P(AXES, None)),
        check_vma=False,
    )
```

```python
import jax
import jax.numpy as jnp
from jax import lax
from jax.experimental import pallas as pl
from jax.experimental.pallas import tpu as pltpu
from jax.sharding import PartitionSpec as P

AXES = ("group", "dp")
SHARP = 1.0 / 0.02
FLOOR = -1e30
BF = jnp.bfloat16
F32 = jnp.float32
WIDTH = 2048
VMEM = pl.BlockSpec(memory_space=pltpu.VMEM)
ANY = pl.BlockSpec(memory_space=pl.ANY)


def index(y, x, z, c):
    return (((y % 4) * 4 + x % 4) * 4 + z % 4) * 2 + c % 2


def pairs(step):
    found = []
    for y in range(4):
        for x in range(4):
            for z in range(4):
                for c in range(2):
                    found.append((index(y, x, z, c), index(*step(y, x, z, c))))
    return found


def first(d):
    return pairs(lambda y, x, z, c: (y, x, z + d, c) if c else (y, x + d, z, c))


def second(d):
    return pairs(lambda y, x, z, c: (y, x + d, z, c) if c else (y, x, z + d, c))


def along(d):
    return pairs(lambda y, x, z, c: (y - d, x, z, c) if c else (y + d, x, z, c))


CORE = pairs(lambda y, x, z, c: (y, x, z, 1 - c))


def send(v, perm):
    return lax.ppermute(v, AXES, perm)


def tied(*v):
    return lax.optimization_barrier(v)


def join(*v):
    return jnp.concatenate(v, axis=0)


def call(kernel, outs, specs, flops=0, nbytes=0, scratch=(), limit=16):
    return pl.pallas_call(
        kernel,
        out_shape=outs,
        in_specs=specs,
        out_specs=jax.tree.map(lambda _: VMEM, outs),
        scratch_shapes=scratch,
        compiler_params=pltpu.CompilerParams(vmem_limit_bytes=limit * 2**20),
        cost_estimate=pl.CostEstimate(flops=flops, bytes_accessed=nbytes, transcendentals=0),
    )


def shape(r, c, t):
    return jax.ShapeDtypeStruct((r, c), t)


def pack_kernel(q_ref, owner_ref, row_ref, pos_ref, out_ref, owner, row, pos, sems):
    copies = []
    for i, (src, dst) in enumerate(
        ((owner_ref, owner), (row_ref, row), (pos_ref, pos), (q_ref, out_ref.at[0:128, :]))
    ):
        copies.append(pltpu.make_async_copy(src, dst, sems.at[i]))
        copies[-1].start()
    out_ref[128:144, 384:WIDTH] = jnp.zeros((16, WIDTH - 384), BF)
    for c in copies[:3]:
        c.wait()
    high = (pos[...] // 64).astype(F32)
    low = (pos[...] % 64).astype(F32)
    third = jnp.concatenate([high, low, jnp.zeros((14, 128), F32)], axis=0)
    meta = jnp.concatenate([owner[...].astype(F32), row[...].astype(F32), third], axis=1)
    out_ref[128:144, 0:384] = meta.astype(BF)
    copies[3].wait()


def stage_kernel(a_ref, b_ref, a_out, b_out, sems):
    one = pltpu.make_async_copy(a_ref, a_out, sems.at[0])
    two = pltpu.make_async_copy(b_ref, b_out, sems.at[1])
    one.start()
    two.start()
    one.wait()
    two.wait()


def join_kernel(*refs):
    for i, r in enumerate(refs[:4]):
        refs[4][64 * i : 64 * i + 64, :] = r[...]


def whereabouts():
    dp = lax.axis_index("dp")
    return lax.axis_index("group"), dp // 8, lax.rem(dp // 2, 4), lax.rem(dp, 2)


def owner_id(place, piece, k1):
    x, z, core = place[1], place[2], place[3]
    kx = jnp.where(core == 0, k1, piece)
    kz = jnp.where(core == 0, piece, k1)
    return (lax.rem(x - kx + 4, 4) * 4 + lax.rem(z - kz + 4, 4)) * 2 + core


PIECES = (0, 1, 2, 3)


def steps(n):
    return lax.broadcasted_iota(jnp.int32, (64, n), 0).astype(F32) + 1.0


def score_block(place, piece, pair, a, b, raw, t_ref, write):
    rows = []
    owners = jnp.concatenate([a[128:144, 0:128], b[128:144, 0:128]], axis=1).astype(F32)
    spots = jnp.concatenate([a[128:144, 128:256], b[128:144, 128:256]], axis=1).astype(F32) + 1.0
    step = steps(256)
    hard, where = [], []
    for k1 in range(4):
        whole = (place[0] * 32 + owner_id(place, piece, k1)).astype(F32)
        spot = jnp.sum(jnp.where(owners == whole, spots, 0.0), axis=0, keepdims=True)
        part = raw[64 * k1 : 64 * k1 + 64]
        found = jnp.sum(jnp.where(step == spot, part, 0.0), axis=0, keepdims=True) * SHARP
        hard.append(jnp.where(spot > 0, found, FLOOR))
        where.append(spot)
    top = jnp.maximum(jnp.maximum(hard[0], hard[1]), jnp.maximum(hard[2], hard[3]))
    chosen = jnp.zeros((1, 256), F32)
    marks = [chosen] * 4
    total = chosen
    if pair == 0:
        scores = raw * SHARP
        top = jnp.maximum(top, jnp.max(scores, axis=0, keepdims=True))
        t = jnp.exp(scores - top)
        t_ref[...] = t
        total = jnp.sum(t, axis=0, keepdims=True)
        pos = jnp.concatenate([a[128:144, 256:384], b[128:144, 256:384]], axis=1).astype(F32)
        marks = []
        for k1 in range(4):
            mine = owner_id(place, piece, k1).astype(F32)
            mark = jnp.where(pos[0:1] == mine, pos[1:2] + 1.0, 0.0)
            part = scores[64 * k1 : 64 * k1 + 64]
            chosen = chosen + jnp.sum(jnp.where(step == mark, part, 0.0), axis=0, keepdims=True)
            marks.append(mark)
    for k1 in range(4):
        total = total + jnp.where(where[k1] > 0, jnp.exp(hard[k1] - top), 0.0)
    write(jnp.concatenate([*hard, *where, top, total, chosen, *marks, jnp.zeros((1, 256), F32)], axis=0))


def product(p, a, b):
    q = jnp.concatenate([a[0:128, :], b[0:128, :]], axis=0)
    return lax.dot_general(p, q, (((1,), (1,)), ((), ())), preferred_element_type=F32)


def writer(ref, rows, cols):
    def write(v):
        ref[rows : rows + 16, cols : cols + 256] = v

    return write


def early_kernel(pieces, *refs):
    p_refs, q_refs, ts, info = refs[0:2], refs[2:8], refs[8:10], refs[10]
    place = whereabouts()
    p = jnp.concatenate([r[...] for r in p_refs], axis=0)
    for pair in range(3):
        a, b = q_refs[2 * pair], q_refs[2 * pair + 1]
        raw = product(p, a, b)
        for i, piece in enumerate(pieces):
            part = raw[256 * i : 256 * i + 256]
            score_block(place, piece, pair, a, b, part, ts[i], writer(info, 16 * i, 256 * pair))


SOON, LATER = (0, 2), (1, 3)


class Info:
    def __init__(self, *refs):
        self.refs = refs

    def rows(self, piece, pair, first, last):
        if pair < 3:
            ref = self.refs[0 if piece in SOON else 1]
            i = 16 * (SOON if piece in SOON else LATER).index(piece)
            return ref[i + first : i + last, 256 * pair : 256 * pair + 256]
        i = 16 * piece
        return self.refs[2][i + first : i + last, 0:256]


def merge(a, b):
    top = jnp.maximum(a[0], b[0])
    total = a[1] * jnp.exp(a[0] - top) + b[1] * jnp.exp(b[0] - top)
    return top, total, a[2] + b[2]


def unpack(v):
    return v[0:1], v[1:2], v[2:3]


def late_kernel(*refs):
    p_refs, q_refs, soon, later, info_b, stats_ref = refs[0:4], refs[4:6], *refs[6:10]
    place = whereabouts()
    p = jnp.concatenate([r[...] for r in p_refs], axis=0)
    raw = product(p, q_refs[0], q_refs[1])
    for i in PIECES:
        part = raw[256 * i : 256 * i + 256]
        score_block(place, i, 3, q_refs[0], q_refs[1], part, None, writer(info_b, 16 * i, 0))
    info = Info(soon, later, info_b)
    for pair in range(4):
        acc = unpack(info.rows(0, pair, 8, 11))
        for piece in (1, 2, 3):
            acc = merge(acc, unpack(info.rows(piece, pair, 8, 11)))
        stats_ref[:, 256 * pair : 256 * pair + 256] = jnp.concatenate([*acc, jnp.zeros((5, 256), F32)], axis=0)


def query_kernel(half, *refs):
    ts, infos, stats, p_refs, out_ref, turned = refs[0:4], refs[4:7], refs[7], refs[8:12], refs[13], refs[14]
    info = Info(*infos)
    step = steps(128)
    side = slice(128 * half, 128 * half + 128)
    for piece in PIECES:
        cols = slice(256 * piece, 256 * piece + 256)
        for pair in range(4):
            top = stats[0:1, 256 * pair + 128 * half : 256 * pair + 128 * half + 128]
            rows = info.rows(piece, pair, 0, 16)[:, side]
            parts = []
            marks = []
            for k1 in range(4):
                part = jnp.where(step == rows[4 + k1 : 5 + k1], jnp.exp(rows[k1 : k1 + 1] - top), 0.0)
                if pair == 0:
                    t = ts[piece][64 * k1 : 64 * k1 + 64, side] * jnp.exp(rows[8:9] - top)
                    mark = step == rows[11 + k1 : 12 + k1]
                    part = part + jnp.where(mark, 0.0, t)
                    marks.append(jnp.where(mark, 1.0, 0.0))
                parts.append(part)
            turned[128 * pair : 128 * pair + 128, cols] = jnp.transpose(jnp.concatenate(parts, axis=0).astype(BF))
            if pair == 0:
                turned[512:640, cols] = jnp.transpose(jnp.concatenate(marks, axis=0).astype(BF))
    for n in range(4):
        cols = slice(512 * n, 512 * n + 512)
        p = jnp.concatenate([r[:, cols] for r in p_refs], axis=0)
        out_ref[:, cols] = jnp.dot(turned[...], p, preferred_element_type=F32).astype(out_ref.dtype)


def swap(v):
    return jnp.concatenate([v[:, 128 * (i ^ 1) : 128 * (i ^ 1) + 128] for i in range(8)], axis=1)


def aligned(v, t):
    picked = []
    for i in range(4):
        j, k = (i - t) % 4, (i + t) % 4
        picked += [v[:, 256 * j : 256 * j + 128], v[:, 256 * k + 128 : 256 * k + 256]]
    return jnp.concatenate(picked, axis=1)


def merge_kernel(t, raw, other, *refs):
    got = aligned(other[...], t) if t else swap(other[...])
    both = merge(unpack(raw[...]), unpack(got))
    refs[-1][...] = jnp.concatenate([*both, jnp.zeros((5, 1024), F32)], axis=0)


def block_kernel(k, mine, theirs, factor, extra, *refs):
    got, out_ref = refs[0], refs[1 if k < 3 else 0]
    if k == 0:
        refs[2][...] = jnp.zeros((8, 128), F32)
        refs[3][...] = extra[1:2, 0:128]
    rows = slice(128 * k, 128 * k + 128)
    f = factor[...]
    for n in range(4):
        cols = slice(512 * n, 512 * n + 512)
        v = mine[rows, cols] * f[:, k : k + 1] + theirs[rows, cols].astype(F32) * f[:, 4 + k : 5 + k]
        if k == 0:
            v = v + (mine[512:640, cols] + theirs[512:640, cols].astype(F32)) * f[:, 8:9]
        if k < 3:
            v = v + got[:, cols].astype(F32)
        out_ref[:, cols] = v.astype(BF)


def gather_kernel(zero, one, two, three, *outs):
    for k in range(4):
        rows = slice(64 * k, 64 * k + 64)
        v = zero[rows] + two[rows].astype(F32) + (one[rows].astype(F32) + three[rows].astype(F32))
        outs[k][...] = v.astype(outs[k].dtype)


def last_kernel(a, b, c, d, _, out_ref):
    v = a[...] + b[...].astype(F32) + (c[...].astype(F32) + d[...].astype(F32))
    out_ref[...] = v.astype(BF)


def total_kernel(raw, other, stats, got, _, lse_ref, factor_ref):
    acc = merge(unpack(stats[...]), unpack(aligned(got[...], 2)))
    lse = acc[0] + jnp.log(acc[1])
    chosen = acc[2][:, 0:128]
    loss = jnp.concatenate([lse[:, 0:128] - chosen, jnp.zeros((1, 896), F32)], axis=1)
    lse_ref[...] = jnp.concatenate([lse, loss, jnp.zeros((6, 1024), F32)], axis=0)
    rows = []
    for top in (raw[0:1, :], swap(other[...])[0:1]):
        f = jnp.exp(top - lse) * SHARP
        rows += [f[:, 256 * j : 256 * j + 128] for j in range(4)]
    pos = ((jnp.exp(chosen - lse[:, 0:128]) - 1.0) * SHARP).astype(BF).astype(F32)
    factor_ref[...] = jnp.transpose(jnp.concatenate([*rows, pos, jnp.zeros((119, 128), F32)], axis=0))


def coefficients(info, piece, t_ref, lse_ref, c_ref, at):
    step = steps(256)
    for pair in range(4):
        cols = slice(256 * pair, 256 * pair + 256)
        lse = lse_ref[0:1, cols]
        rows = info.rows(piece, pair, 0, 16)
        parts = []
        for k1 in range(4):
            part = jnp.where(step == rows[4 + k1 : 5 + k1], jnp.exp(rows[k1 : k1 + 1] - lse) * SHARP, 0.0)
            if pair == 0:
                t = t_ref[64 * k1 : 64 * k1 + 64, :] * jnp.exp(rows[8:9] - lse)
                t = t - jnp.where(step == rows[11 + k1 : 12 + k1], 1.0, 0.0)
                part = part + t * SHARP
            parts.append(part)
        c_ref[at : at + 256, cols] = jnp.concatenate(parts, axis=0).astype(BF)


def far_kernel(t_ref, *refs):
    infos, lse_ref, q_refs = refs[0:3], refs[3], refs[4:12]
    out_ref, c = refs[12:]
    coefficients(Info(*infos), 2, t_ref, lse_ref, c, 0)
    for n in range(4):
        cols = slice(512 * n, 512 * n + 512)
        q = jnp.concatenate([r[0:128, cols] for r in q_refs], axis=0)
        out_ref[:, cols] = jnp.dot(c[...], q, preferred_element_type=F32).astype(BF)


def near_kernel(*refs):
    ts, infos, lse_ref, q_refs = refs[0:3], refs[3:6], refs[6], refs[7:15]
    zero, one, three, c = refs[16:]
    info = Info(*infos)
    for i, piece in enumerate((0, 1, 3)):
        coefficients(info, piece, ts[i], lse_ref, c, 256 * i)
    for n in range(4):
        cols = slice(512 * n, 512 * n + 512)
        q = jnp.concatenate([r[0:128, cols] for r in q_refs], axis=0)
        g = jnp.dot(c[...], q, preferred_element_type=F32)
        zero[:, cols] = g[0:256]
        one[:, cols] = g[256:512].astype(BF)
        three[:, cols] = g[512:768].astype(BF)


def local(question_vectors, passages, positive, hard_owner, hard_row):
    packed = call(
        pack_kernel,
        shape(144, WIDTH, BF),
        [ANY] * 4,
        scratch=[
            pltpu.VMEM((16, 128), jnp.int32),
            pltpu.VMEM((16, 128), jnp.int32),
            pltpu.VMEM((1, 128), jnp.int32),
            pltpu.SemaphoreType.DMA((4,)),
        ],
        limit=56,
    )(question_vectors, hard_owner.T, hard_row.T, positive.reshape(1, 128))

    back = send(passages, first(1))
    ahead = send(passages, first(-1))
    across = send(passages, first(2))
    q1 = send(packed, along(1))
    mine0, kept = call(
        stage_kernel,
        (shape(144, WIDTH, BF), shape(64, WIDTH, BF)),
        [ANY, ANY],
        scratch=[pltpu.SemaphoreType.DMA((2,))],
    )(packed, passages)
    s0 = send(packed, CORE)
    across, back, ahead, s0 = tied(across, back, ahead, s0)
    plane = call(join_kernel, shape(256, WIDTH, BF), [VMEM] * 4)(kept, back, across, ahead)
    up = send(plane, second(1))
    down = send(plane, second(-1))
    over = send(plane, second(2))
    q2 = send(q1, along(1))
    q2, q1 = tied(q2, q1)
    s1 = send(q1, CORE)
    q3 = send(q2, along(1))
    s2 = send(q2, CORE)
    s3 = send(q3, CORE)
    tiles = (mine0, s0, q1, s1, q2, s2, q3, s3)

    pieces = (plane, up, over, down)
    tile = shape(256, 256, F32)

    def early(which):
        return call(
            lambda *r: early_kernel(which, *r),
            (tile, tile, shape(32, 768, F32)),
            [VMEM] * 8,
            2 * 512 * 768 * WIDTH,
        )(*[pieces[i] for i in which], *tiles[:6])

    t0, t2, soon = early(SOON)
    t1, t3, later = early(LATER)
    info_b, raw = call(
        late_kernel, (shape(64, 256, F32), shape(8, 1024, F32)), [VMEM] * 8, 2 * 1024 * 256 * WIDTH
    )(*pieces, *tiles[6:], soon, later)

    other = send(raw, CORE)
    stats = call(lambda *r: merge_kernel(0, *r), shape(8, 1024, F32), [VMEM] * 2)(raw, other)
    infos = (soon, later, info_b)
    operands = (t0, t1, t2, t3, *infos, raw, *pieces)

    def query(half, kind, after):
        return call(
            lambda *r: query_kernel(half, *r),
            shape(640, WIDTH, kind),
            [VMEM] * 13,
            2 * 640 * 1024 * WIDTH,
            scratch=[pltpu.VMEM((640, 1024), BF)],
        )(*operands, after)

    mine = query(0, F32, stats)
    both = call(lambda *r: merge_kernel(1, *r), shape(8, 1024, F32), [VMEM] * 3)(stats, send(stats, along(1)), mine)
    four = send(both, along(2))
    theirs = query(1, BF, both)
    lse, factor = call(
        total_kernel, (shape(8, 1024, F32), shape(128, 128, F32)), [VMEM] * 5
    )(raw, other, both, four, theirs)
    theirs, lse = tied(theirs, lse)
    theirs = send(theirs, CORE)

    far = call(far_kernel, shape(256, WIDTH, BF), [VMEM] * 13, 2 * 256 * 1024 * WIDTH, scratch=[pltpu.VMEM((256, 1024), BF)])(
        t2, *infos, lse, *tiles
    )
    two = send(far, second(2))

    zero, one, three = call(
        near_kernel,
        (shape(256, WIDTH, F32), shape(256, WIDTH, BF), shape(256, WIDTH, BF)),
        [VMEM] * 16,
        2 * 768 * 1024 * WIDTH,
        scratch=[pltpu.VMEM((768, 1024), BF)],
    )(t0, t1, t3, *infos, lse, *tiles, theirs)
    def block(k, *got):
        kernel = lambda *r: block_kernel(k, *r)
        outs = (shape(128, WIDTH, BF), shape(8, 128, F32), shape(1, 128, F32)) if k == 0 else shape(128, WIDTH, BF)
        return call(kernel, outs, [VMEM] * (4 + len(got)))(mine, theirs, factor, lse, *got)

    run = block(3)
    for k in (2, 1, 0):
        run = block(k, send(run, along(-1)))
    run, token, loss = run

    one = send(one, second(-1))
    three = send(three, second(1))
    half = shape(64, WIDTH, BF)
    g0, g1, g2, g3 = call(gather_kernel, (shape(64, WIDTH, F32), half, half, half), [VMEM] * 4)(zero, one, two, three)
    g2 = send(g2, first(2))
    g1 = send(g1, first(-1))
    g3 = send(g3, first(1))
    passage_grad = call(last_kernel, half, [VMEM] * 5)(g0, g2, g1, g3, token)
    return loss.reshape(128), run, passage_grad


def solution(mesh):
    return jax.shard_map(
        local,
        mesh=mesh,
        in_specs=(P(AXES, None), P(AXES, None), P(AXES), P(AXES, None), P(AXES, None)),
        out_specs=(P(AXES), P(AXES, None), P(AXES, None)),
        check_vma=False,
    )
```

```python
import jax
import jax.numpy as jnp
from jax import lax
from jax.experimental import pallas as pl
from jax.experimental.pallas import tpu as pltpu
from jax.sharding import PartitionSpec as P

AXES = ("group", "dp")
SHARP = 1.0 / 0.02
FLOOR = -1e30
BF = jnp.bfloat16
F32 = jnp.float32
WIDTH = 2048
VMEM = pl.BlockSpec(memory_space=pltpu.VMEM)
ANY = pl.BlockSpec(memory_space=pl.ANY)


def index(y, x, z, c):
    return (((y % 4) * 4 + x % 4) * 4 + z % 4) * 2 + c % 2


def pairs(step):
    found = []
    for y in range(4):
        for x in range(4):
            for z in range(4):
                for c in range(2):
                    found.append((index(y, x, z, c), index(*step(y, x, z, c))))
    return found


def first(d):
    return pairs(lambda y, x, z, c: (y, x, z + d, c) if c else (y, x + d, z, c))


def second(d):
    return pairs(lambda y, x, z, c: (y, x + d, z, c) if c else (y, x, z + d, c))


def along(d):
    return pairs(lambda y, x, z, c: (y - d, x, z, c) if c else (y + d, x, z, c))


CORE = pairs(lambda y, x, z, c: (y, x, z, 1 - c))


def send(v, perm):
    return lax.ppermute(v, AXES, perm)


def tied(*v):
    return lax.optimization_barrier(v)


def join(*v):
    return jnp.concatenate(v, axis=0)


def call(kernel, outs, specs, flops=0, nbytes=0, scratch=(), limit=16):
    return pl.pallas_call(
        kernel,
        out_shape=outs,
        in_specs=specs,
        out_specs=jax.tree.map(lambda _: VMEM, outs),
        scratch_shapes=scratch,
        compiler_params=pltpu.CompilerParams(vmem_limit_bytes=limit * 2**20),
        cost_estimate=pl.CostEstimate(flops=flops, bytes_accessed=nbytes, transcendentals=0),
    )


def shape(r, c, t):
    return jax.ShapeDtypeStruct((r, c), t)


def pack_kernel(q_ref, owner_ref, row_ref, pos_ref, out_ref, owner, row, pos, sems):
    copies = []
    for i, (src, dst) in enumerate(
        ((owner_ref, owner), (row_ref, row), (pos_ref, pos), (q_ref, out_ref.at[0:128, :]))
    ):
        copies.append(pltpu.make_async_copy(src, dst, sems.at[i]))
        copies[-1].start()
    out_ref[128:144, 384:WIDTH] = jnp.zeros((16, WIDTH - 384), BF)
    for c in copies[:3]:
        c.wait()
    high = (pos[...] // 64).astype(F32)
    low = (pos[...] % 64).astype(F32)
    third = jnp.concatenate([high, low, jnp.zeros((14, 128), F32)], axis=0)
    meta = jnp.concatenate([owner[...].astype(F32), row[...].astype(F32), third], axis=1)
    out_ref[128:144, 0:384] = meta.astype(BF)
    copies[3].wait()


def stage_kernel(a_ref, b_ref, a_out, b_out, sems):
    one = pltpu.make_async_copy(a_ref, a_out, sems.at[0])
    two = pltpu.make_async_copy(b_ref, b_out, sems.at[1])
    one.start()
    two.start()
    one.wait()
    two.wait()


def join_kernel(*refs):
    for i, r in enumerate(refs[:4]):
        refs[4][64 * i : 64 * i + 64, :] = r[...]


def whereabouts():
    dp = lax.axis_index("dp")
    return lax.axis_index("group"), dp // 8, lax.rem(dp // 2, 4), lax.rem(dp, 2)


def owner_id(place, piece, k1):
    x, z, core = place[1], place[2], place[3]
    kx = jnp.where(core == 0, k1, piece)
    kz = jnp.where(core == 0, piece, k1)
    return (lax.rem(x - kx + 4, 4) * 4 + lax.rem(z - kz + 4, 4)) * 2 + core


PIECES = (0, 1, 2, 3)


def steps(n):
    return lax.broadcasted_iota(jnp.int32, (64, n), 0).astype(F32) + 1.0


def score_block(place, piece, pair, a, b, raw, t_ref, write):
    rows = []
    owners = jnp.concatenate([a[128:144, 0:128], b[128:144, 0:128]], axis=1).astype(F32)
    spots = jnp.concatenate([a[128:144, 128:256], b[128:144, 128:256]], axis=1).astype(F32) + 1.0
    step = steps(256)
    hard, where = [], []
    for k1 in range(4):
        whole = (place[0] * 32 + owner_id(place, piece, k1)).astype(F32)
        spot = jnp.sum(jnp.where(owners == whole, spots, 0.0), axis=0, keepdims=True)
        part = raw[64 * k1 : 64 * k1 + 64]
        found = jnp.sum(jnp.where(step == spot, part, 0.0), axis=0, keepdims=True) * SHARP
        hard.append(jnp.where(spot > 0, found, FLOOR))
        where.append(spot)
    top = jnp.maximum(jnp.maximum(hard[0], hard[1]), jnp.maximum(hard[2], hard[3]))
    chosen = jnp.zeros((1, 256), F32)
    marks = [chosen] * 4
    total = chosen
    if pair == 0:
        scores = raw * SHARP
        top = jnp.maximum(top, jnp.max(scores, axis=0, keepdims=True))
        t = jnp.exp(scores - top)
        t_ref[...] = t
        total = jnp.sum(t, axis=0, keepdims=True)
        pos = jnp.concatenate([a[128:144, 256:384], b[128:144, 256:384]], axis=1).astype(F32)
        marks = []
        for k1 in range(4):
            mine = owner_id(place, piece, k1).astype(F32)
            mark = jnp.where(pos[0:1] == mine, pos[1:2] + 1.0, 0.0)
            part = scores[64 * k1 : 64 * k1 + 64]
            chosen = chosen + jnp.sum(jnp.where(step == mark, part, 0.0), axis=0, keepdims=True)
            marks.append(mark)
    for k1 in range(4):
        total = total + jnp.where(where[k1] > 0, jnp.exp(hard[k1] - top), 0.0)
    write(jnp.concatenate([*hard, *where, top, total, chosen, *marks, jnp.zeros((1, 256), F32)], axis=0))


def product(p, a, b):
    q = jnp.concatenate([a[0:128, :], b[0:128, :]], axis=0)
    return lax.dot_general(p, q, (((1,), (1,)), ((), ())), preferred_element_type=F32)


def writer(ref, rows, cols):
    def write(v):
        ref[rows : rows + 16, cols : cols + 256] = v

    return write


def early_kernel(pieces, *refs):
    p_refs, q_refs, ts, info = refs[0:2], refs[2:8], refs[8:10], refs[10]
    place = whereabouts()
    p = jnp.concatenate([r[...] for r in p_refs], axis=0)
    for pair in range(3):
        a, b = q_refs[2 * pair], q_refs[2 * pair + 1]
        raw = product(p, a, b)
        for i, piece in enumerate(pieces):
            part = raw[256 * i : 256 * i + 256]
            score_block(place, piece, pair, a, b, part, ts[i], writer(info, 16 * i, 256 * pair))


SOON, LATER = (0, 2), (1, 3)


class Info:
    def __init__(self, *refs):
        self.refs = refs

    def rows(self, piece, pair, first, last):
        if pair < 3:
            ref = self.refs[0 if piece in SOON else 1]
            i = 16 * (SOON if piece in SOON else LATER).index(piece)
            return ref[i + first : i + last, 256 * pair : 256 * pair + 256]
        i = 16 * piece
        return self.refs[2][i + first : i + last, 0:256]


def merge(a, b):
    top = jnp.maximum(a[0], b[0])
    total = a[1] * jnp.exp(a[0] - top) + b[1] * jnp.exp(b[0] - top)
    return top, total, a[2] + b[2]


def unpack(v):
    return v[0:1], v[1:2], v[2:3]


def late_kernel(*refs):
    p_refs, q_refs, soon, later, info_b, stats_ref = refs[0:4], refs[4:6], *refs[6:10]
    place = whereabouts()
    p = jnp.concatenate([r[...] for r in p_refs], axis=0)
    raw = product(p, q_refs[0], q_refs[1])
    for i in PIECES:
        part = raw[256 * i : 256 * i + 256]
        score_block(place, i, 3, q_refs[0], q_refs[1], part, None, writer(info_b, 16 * i, 0))
    info = Info(soon, later, info_b)
    for pair in range(4):
        acc = unpack(info.rows(0, pair, 8, 11))
        for piece in (1, 2, 3):
            acc = merge(acc, unpack(info.rows(piece, pair, 8, 11)))
        stats_ref[:, 256 * pair : 256 * pair + 256] = jnp.concatenate([*acc, jnp.zeros((5, 256), F32)], axis=0)


def query_kernel(half, *refs):
    ts, infos, stats, p_refs, out_ref, turned = refs[0:4], refs[4:7], refs[7], refs[8:12], refs[13], refs[14]
    info = Info(*infos)
    step = steps(128)
    side = slice(128 * half, 128 * half + 128)
    for piece in PIECES:
        cols = slice(256 * piece, 256 * piece + 256)
        for pair in range(4):
            top = stats[0:1, 256 * pair + 128 * half : 256 * pair + 128 * half + 128]
            rows = info.rows(piece, pair, 0, 16)[:, side]
            parts = []
            marks = []
            for k1 in range(4):
                part = jnp.where(step == rows[4 + k1 : 5 + k1], jnp.exp(rows[k1 : k1 + 1] - top), 0.0)
                if pair == 0:
                    t = ts[piece][64 * k1 : 64 * k1 + 64, side] * jnp.exp(rows[8:9] - top)
                    mark = step == rows[11 + k1 : 12 + k1]
                    part = part + jnp.where(mark, 0.0, t)
                    marks.append(jnp.where(mark, 1.0, 0.0))
                parts.append(part)
            turned[128 * pair : 128 * pair + 128, cols] = jnp.transpose(jnp.concatenate(parts, axis=0).astype(BF))
            if pair == 0:
                turned[512:640, cols] = jnp.transpose(jnp.concatenate(marks, axis=0).astype(BF))
    for n in range(4):
        cols = slice(512 * n, 512 * n + 512)
        p = jnp.concatenate([r[:, cols] for r in p_refs], axis=0)
        out_ref[:, cols] = jnp.dot(turned[...], p, preferred_element_type=F32).astype(out_ref.dtype)


def swap(v):
    return jnp.concatenate([v[:, 128 * (i ^ 1) : 128 * (i ^ 1) + 128] for i in range(8)], axis=1)


def aligned(v, t):
    picked = []
    for i in range(4):
        j, k = (i - t) % 4, (i + t) % 4
        picked += [v[:, 256 * j : 256 * j + 128], v[:, 256 * k + 128 : 256 * k + 256]]
    return jnp.concatenate(picked, axis=1)


def merge_kernel(t, raw, other, *refs):
    got = aligned(other[...], t) if t else swap(other[...])
    both = merge(unpack(raw[...]), unpack(got))
    refs[-1][...] = jnp.concatenate([*both, jnp.zeros((5, 1024), F32)], axis=0)


def block_kernel(k, mine, theirs, factor, extra, *refs):
    got, out_ref = refs[0], refs[1 if k < 3 else 0]
    if k == 0:
        refs[2][...] = jnp.zeros((8, 128), F32)
        refs[3][...] = extra[1:2, 0:128]
    rows = slice(128 * k, 128 * k + 128)
    f = factor[...]
    for n in range(4):
        cols = slice(512 * n, 512 * n + 512)
        v = mine[rows, cols] * f[:, k : k + 1] + theirs[rows, cols].astype(F32) * f[:, 4 + k : 5 + k]
        if k == 0:
            v = v + (mine[512:640, cols] + theirs[512:640, cols].astype(F32)) * f[:, 8:9]
        if k < 3:
            v = v + got[:, cols].astype(F32)
        out_ref[:, cols] = v.astype(BF)


def gather_kernel(zero, one, two, three, *outs):
    for k in range(4):
        rows = slice(64 * k, 64 * k + 64)
        v = zero[rows] + two[rows].astype(F32) + (one[rows].astype(F32) + three[rows].astype(F32))
        outs[k][...] = v.astype(outs[k].dtype)


def last_kernel(a, b, c, d, _, out_ref):
    v = a[...] + b[...].astype(F32) + (c[...].astype(F32) + d[...].astype(F32))
    out_ref[...] = v.astype(BF)


def total_kernel(raw, other, stats, got, _, lse_ref, factor_ref):
    acc = merge(unpack(stats[...]), unpack(aligned(got[...], 2)))
    lse = acc[0] + jnp.log(acc[1])
    chosen = acc[2][:, 0:128]
    loss = jnp.concatenate([lse[:, 0:128] - chosen, jnp.zeros((1, 896), F32)], axis=1)
    lse_ref[...] = jnp.concatenate([lse, loss, jnp.zeros((6, 1024), F32)], axis=0)
    rows = []
    for top in (raw[0:1, :], swap(other[...])[0:1]):
        f = jnp.exp(top - lse) * SHARP
        rows += [f[:, 256 * j : 256 * j + 128] for j in range(4)]
    pos = ((jnp.exp(chosen - lse[:, 0:128]) - 1.0) * SHARP).astype(BF).astype(F32)
    factor_ref[...] = jnp.transpose(jnp.concatenate([*rows, pos, jnp.zeros((119, 128), F32)], axis=0))


def coefficients(info, piece, t_ref, lse_ref, c_ref, at):
    step = steps(256)
    for pair in range(4):
        cols = slice(256 * pair, 256 * pair + 256)
        lse = lse_ref[0:1, cols]
        rows = info.rows(piece, pair, 0, 16)
        parts = []
        for k1 in range(4):
            part = jnp.where(step == rows[4 + k1 : 5 + k1], jnp.exp(rows[k1 : k1 + 1] - lse) * SHARP, 0.0)
            if pair == 0:
                t = t_ref[64 * k1 : 64 * k1 + 64, :] * jnp.exp(rows[8:9] - lse)
                t = t - jnp.where(step == rows[11 + k1 : 12 + k1], 1.0, 0.0)
                part = part + t * SHARP
            parts.append(part)
        c_ref[at : at + 256, cols] = jnp.concatenate(parts, axis=0).astype(BF)


def far_kernel(t_ref, *refs):
    infos, lse_ref, q_refs = refs[0:3], refs[3], refs[4:12]
    out_ref, c = refs[12:]
    coefficients(Info(*infos), 2, t_ref, lse_ref, c, 0)
    for n in range(4):
        cols = slice(512 * n, 512 * n + 512)
        q = jnp.concatenate([r[0:128, cols] for r in q_refs], axis=0)
        out_ref[:, cols] = jnp.dot(c[...], q, preferred_element_type=F32).astype(BF)


def near_kernel(*refs):
    ts, infos, lse_ref, q_refs = refs[0:3], refs[3:6], refs[6], refs[7:15]
    zero, one, three, c = refs[16:]
    info = Info(*infos)
    for i, piece in enumerate((0, 1, 3)):
        coefficients(info, piece, ts[i], lse_ref, c, 256 * i)
    for n in range(4):
        cols = slice(512 * n, 512 * n + 512)
        q = jnp.concatenate([r[0:128, cols] for r in q_refs], axis=0)
        g = jnp.dot(c[...], q, preferred_element_type=F32)
        zero[:, cols] = g[0:256]
        one[:, cols] = g[256:512].astype(BF)
        three[:, cols] = g[512:768].astype(BF)


def local(question_vectors, passages, positive, hard_owner, hard_row):
    packed = call(
        pack_kernel,
        shape(144, WIDTH, BF),
        [ANY] * 4,
        scratch=[
            pltpu.VMEM((16, 128), jnp.int32),
            pltpu.VMEM((16, 128), jnp.int32),
            pltpu.VMEM((1, 128), jnp.int32),
            pltpu.SemaphoreType.DMA((4,)),
        ],
        limit=56,
    )(question_vectors, hard_owner.T, hard_row.T, positive.reshape(1, 128))

    back = send(passages, first(1))
    ahead = send(passages, first(-1))
    across = send(passages, first(2))
    q1 = send(packed, along(1))
    mine0, kept = call(
        stage_kernel,
        (shape(144, WIDTH, BF), shape(64, WIDTH, BF)),
        [ANY, ANY],
        scratch=[pltpu.SemaphoreType.DMA((2,))],
    )(packed, passages)
    s0 = send(packed, CORE)
    across, ahead, back, s0 = tied(across, ahead, back, s0)
    plane = call(join_kernel, shape(256, WIDTH, BF), [VMEM] * 4)(kept, back, across, ahead)
    up = send(plane, second(1))
    down = send(plane, second(-1))
    over = send(plane, second(2))
    q2 = send(q1, along(1))
    q2, q1 = tied(q2, q1)
    s1 = send(q1, CORE)
    q3 = send(q2, along(1))
    s2 = send(q2, CORE)
    s3 = send(q3, CORE)
    tiles = (mine0, s0, q1, s1, q2, s2, q3, s3)

    pieces = (plane, up, over, down)
    tile = shape(256, 256, F32)

    def early(which):
        return call(
            lambda *r: early_kernel(which, *r),
            (tile, tile, shape(32, 768, F32)),
            [VMEM] * 8,
            2 * 512 * 768 * WIDTH,
        )(*[pieces[i] for i in which], *tiles[:6])

    t0, t2, soon = early(SOON)
    t1, t3, later = early(LATER)
    info_b, raw = call(
        late_kernel, (shape(64, 256, F32), shape(8, 1024, F32)), [VMEM] * 8, 2 * 1024 * 256 * WIDTH
    )(*pieces, *tiles[6:], soon, later)

    other = send(raw, CORE)
    stats = call(lambda *r: merge_kernel(0, *r), shape(8, 1024, F32), [VMEM] * 2)(raw, other)
    infos = (soon, later, info_b)
    operands = (t0, t1, t2, t3, *infos, raw, *pieces)

    def query(half, kind, after):
        return call(
            lambda *r: query_kernel(half, *r),
            shape(640, WIDTH, kind),
            [VMEM] * 13,
            2 * 640 * 1024 * WIDTH,
            scratch=[pltpu.VMEM((640, 1024), BF)],
        )(*operands, after)

    mine = query(0, F32, stats)
    both = call(lambda *r: merge_kernel(1, *r), shape(8, 1024, F32), [VMEM] * 3)(stats, send(stats, along(1)), mine)
    four = send(both, along(2))
    theirs = query(1, BF, both)
    lse, factor = call(
        total_kernel, (shape(8, 1024, F32), shape(128, 128, F32)), [VMEM] * 5
    )(raw, other, both, four, theirs)
    theirs, lse = tied(theirs, lse)
    theirs = send(theirs, CORE)

    far = call(far_kernel, shape(256, WIDTH, BF), [VMEM] * 13, 2 * 256 * 1024 * WIDTH, scratch=[pltpu.VMEM((256, 1024), BF)])(
        t2, *infos, lse, *tiles
    )
    two = send(far, second(2))

    zero, one, three = call(
        near_kernel,
        (shape(256, WIDTH, F32), shape(256, WIDTH, BF), shape(256, WIDTH, BF)),
        [VMEM] * 16,
        2 * 768 * 1024 * WIDTH,
        scratch=[pltpu.VMEM((768, 1024), BF)],
    )(t0, t1, t3, *infos, lse, *tiles, theirs)
    def block(k, *got):
        kernel = lambda *r: block_kernel(k, *r)
        outs = (shape(128, WIDTH, BF), shape(8, 128, F32), shape(1, 128, F32)) if k == 0 else shape(128, WIDTH, BF)
        return call(kernel, outs, [VMEM] * (4 + len(got)))(mine, theirs, factor, lse, *got)

    run = block(3)
    for k in (2, 1, 0):
        run = block(k, send(run, along(-1)))
    run, token, loss = run

    one = send(one, second(-1))
    three = send(three, second(1))
    half = shape(64, WIDTH, BF)
    g0, g1, g2, g3 = call(gather_kernel, (shape(64, WIDTH, F32), half, half, half), [VMEM] * 4)(zero, one, two, three)
    g2 = send(g2, first(2))
    g1 = send(g1, first(-1))
    g3 = send(g3, first(1))
    passage_grad = call(last_kernel, half, [VMEM] * 5)(g0, g2, g3, g1, token)
    return loss.reshape(128), run, passage_grad


def solution(mesh):
    return jax.shard_map(
        local,
        mesh=mesh,
        in_specs=(P(AXES, None), P(AXES, None), P(AXES), P(AXES, None), P(AXES, None)),
        out_specs=(P(AXES), P(AXES, None), P(AXES, None)),
        check_vma=False,
    )
```
